32 devices in a mesh: parts: 2 (over x), tm: 16 (over z, y, core).
Axes of the slice: x: 2, y: 2, z: 4, core: 2. Of those that a mesh axis runs over, the one named last changes fastest.
Arguments:
- observations: float32 [256, 2048], P(('parts', 'tm')), parts along dimension 0, may hold values from -6 to 6
- outage_mask: int32 [256, 16], P(('parts', 'tm')), parts along dimension 0, may hold values 0 or 1
- group_length: int32 [32], P(('parts', 'tm')), parts along dimension 0, may hold values from 1 to 8, 96 in all
- prior_mean: float32 [4096], P('parts'), parts along dimension 0, may hold values from -8 to 8
- transition: float32 [16, 128, 128], replicated, may hold values from -1 to 1, as said below
- filter_gain: float32 [16, 128, 128], replicated, may hold values from -1 to 1, as said below
- smoother_gain: float32 [16, 128, 128], replicated, may hold values from -1 to 1, as said below
Outputs:
- smoothed: float32 [256, 2048], P(('parts', 'tm')), parts along dimension 0
The draws below stay inside these ranges and needn't reach their ends.
There are 2 independent parts, one for each index of `parts`. The reference program is written for one: setup_inputs(seed, part) draws one part's arguments, and reference() takes and returns one part's arrays. A program takes and returns all parts, laid end to end along the dimension named above; an argument that names none is the same for every part. Nothing has to cross between parts.
Inputs may be any that keep to these rules, and one draw needn't show every extreme that they name: `group_length`: live steps of each tm index; they sum to 96 and one entry equals 8. `transition`: nonzero only between states 2p and 2p + 1 of a block; spectral norm below 1. `filter_gain`: Symmetric, eigenvalues between 0 and 1. `smoother_gain`: spectral norm below 1.
All inputs are finite; a program needn't handle non-finite values. No bound on the sum of `outage_mask` or of `group_length` on one device may be relied on, other than what follows from the above.
Results may differ from the reference program's by a relative error of at most 0.0003.
Values sent between devices are 32-bit elements; how exact they have to be, the bound alone decides.
No kernel may reach another device: no remote copies, remote signals or barrier semaphores. Data moves between devices by JAX's collectives and lax.ppermute only.
A program may use at most 320 MiB of HBM per device.

```python
import math
import jax
import jax.numpy as jnp
import numpy as np
from jax import lax

STATES = 2048
BLOCK = 128
CAP = 8
NBLK = 16
SLOTS = 128
N_TM = 16


def one_order(one_key):
    return jax.random.permutation(one_key, BLOCK // 2)


def pair_positions(key):
    keys = jax.random.split(jax.random.fold_in(key, 505), NBLK)
    orders = jax.vmap(one_order)(keys).astype(jnp.int32)
    inverse = jnp.argsort(orders, axis=1).astype(jnp.int32)
    within = jnp.arange(2, dtype=jnp.int32)
    return (2 * inverse[:, :, None] + within[None, None, :]).reshape(NBLK, BLOCK)


def mixed_rates(key, upper_rate, set_size):
    lower_rate = 0.2 / SLOTS
    span = jnp.log(jnp.float32(upper_rate / lower_rate))
    if set_size < BLOCK:
        level_draw = jax.random.uniform(jax.random.fold_in(key, 101), (NBLK, BLOCK // set_size), jnp.float32)
        factor = jax.random.uniform(jax.random.fold_in(key, 102), (NBLK, BLOCK), jnp.float32, 1.0, 2.0)
        levels = lower_rate * jnp.exp(level_draw * span)
        return jnp.repeat(levels, set_size, axis=1) * factor
    uniform_draw = jax.random.uniform(jax.random.fold_in(key, 101), (NBLK, BLOCK), jnp.float32)
    return lower_rate * jnp.exp(uniform_draw * span)


def section_angles(key, salt, section):
    return jax.random.uniform(jax.random.fold_in(key, salt + section), (NBLK, BLOCK), jnp.float32, 0.35, 1.2)


def turn_rows(matrix, angles, section):
    index_row = jnp.arange(BLOCK, dtype=jnp.int32)
    partner = jnp.bitwise_xor(index_row, 1 << section)
    lower = jnp.minimum(index_row, partner)
    chosen = angles[:, lower]
    signs = jnp.where(index_row < partner, -1.0, 1.0).astype(jnp.float32)
    cosine = jnp.cos(chosen)[:, :, None]
    sine_part = (signs[None, :] * jnp.sin(chosen))[:, :, None]
    return cosine * matrix + sine_part * matrix[:, partner, :]


def turn_columns(matrix, angles, section):
    index_row = jnp.arange(BLOCK, dtype=jnp.int32)
    partner = jnp.bitwise_xor(index_row, 1 << section)
    lower = jnp.minimum(index_row, partner)
    chosen = angles[:, lower]
    signs = jnp.where(index_row < partner, -1.0, 1.0).astype(jnp.float32)
    cosine = jnp.cos(chosen)[:, None, :]
    sine_part = (signs[None, :] * jnp.sin(chosen))[:, None, :]
    return cosine * matrix + sine_part * matrix[:, :, partner]


def reorder(matrix, positions):
    return matrix[positions][:, positions]


def spread(key, values, left_salt, right_salt, set_size):
    eye_mask = jnp.eye(BLOCK, dtype=jnp.float32) > 0.5
    matrix = jnp.where(eye_mask[None], values[:, :, None], jnp.float32(0.0))
    for section in range(set_size.bit_length() - 1):
        matrix = turn_rows(matrix, section_angles(key, left_salt, section), section)
        matrix = turn_columns(matrix, section_angles(key, right_salt, section), section)
    return jax.vmap(reorder)(matrix, pair_positions(key))


def draw_transition(key, part):
    upper_rate = 0.25
    set_size = BLOCK // 4
    rates_mixed = mixed_rates(key, upper_rate, set_size)
    rates_state = jnp.take_along_axis(rates_mixed, pair_positions(key), axis=1)
    angles = jax.random.uniform(jax.random.fold_in(key, 202), (NBLK, BLOCK // 2), jnp.float32, 0.3, 1.2)
    scales = 1.0 - rates_state[:, 0::2]
    cosine = scales * jnp.cos(angles)
    sine_part = scales * jnp.sin(angles)
    index_row = jnp.arange(BLOCK)
    pair_index = index_row // 2
    is_even = index_row % 2 == 0
    cos_rows = cosine[:, pair_index]
    sin_rows = sine_part[:, pair_index]
    same_pair = pair_index[:, None] == pair_index[None, :]
    diagonal_mask = index_row[:, None] == index_row[None, :]
    off_entries = jnp.where(is_even[None, :, None], -sin_rows[:, :, None], sin_rows[:, :, None])
    entries = jnp.where(diagonal_mask[None], cos_rows[:, :, None], off_entries)
    return jnp.where(same_pair[None], entries, jnp.float32(0.0))


def draw_filter_gain(key, part):
    upper_rate = 0.25
    set_size = BLOCK // 4
    rates_mixed = mixed_rates(key, upper_rate, set_size)
    matrix = spread(key, rates_mixed, 300, 300, set_size)
    return 0.5 * (matrix + jnp.swapaxes(matrix, 1, 2))


def draw_smoother_gain(key, part):
    upper_rate = 0.25
    set_size = BLOCK // 4
    rates_mixed = mixed_rates(key, upper_rate, set_size)
    return spread(key, 1.0 - rates_mixed, 400, 450, set_size)


def with_ends(drawn, stream_key, smallest, top_value):
    shape = drawn.shape
    place = [jax.random.randint(jax.random.fold_in(stream_key, axis), (), 0, shape[axis]) for axis in range(len(shape))]
    drawn = drawn.at[tuple(place)].set(smallest)
    longest = shape.index(max(shape))
    place[longest] = (place[longest] + 1) % shape[longest]
    return drawn.at[tuple(place)].set(top_value)


def block_levels(own_key, dims, cuts, least, top_value):
    def one(axis_at, blocks):
        steps = jax.random.uniform(jax.random.fold_in(jax.random.fold_in(own_key, 6), axis_at), (blocks,), jnp.float32, least / len(cuts), top_value / len(cuts))
        return jnp.repeat(jnp.exp(steps), dims[axis_at] // blocks).reshape((-1,) + (1,) * (len(dims) - axis_at - 1))

    level = one(*cuts[0])
    for cut in cuts[1:]:
        level = level * one(*cut)
    return level


def profile(number_of, total, bound, slope):
    loads = [(1 << 20) // math.isqrt(grade ** slope) + 1 for grade in range(2, number_of + 1)]
    surplus, counts = total - bound - (number_of - 1), [1] * (number_of - 1)
    while surplus > 0:
        candidates = [i for i in range(number_of - 1) if counts[i] < bound]
        whole, remaining = sum([loads[i] for i in candidates]), surplus
        for i in candidates:
            addition = min(bound - counts[i], max(1, remaining * loads[i] // whole), surplus)
            counts[i] = counts[i] + addition
            surplus = surplus - addition
    return np.array([bound] + counts)


def ragged(key, number_of, total, bound, skew):
    if number_of == 2:
        one = jax.random.randint(key, (), max(1, total - bound), min(bound, total - 1) + 1)
        return jnp.stack([one, total - one])
    sizes = jnp.asarray(profile(number_of, total, bound, skew), jnp.int32)
    pairs = (number_of - 1) // 2
    donor, sink = sizes[1:1 + 2 * pairs:2], sizes[2:2 + 2 * pairs:2]
    margin = jnp.minimum(donor - 1, bound - sink)
    moved = jax.random.randint(jax.random.fold_in(key, 1), (pairs,), 0, 1 << 20) % (margin + 1)
    sizes = sizes.at[1:1 + 2 * pairs:2].set(donor - moved).at[2:2 + 2 * pairs:2].set(sink + moved)
    return sizes[jax.random.permutation(jax.random.fold_in(key, 2), number_of)]


def noise(key, dims, scale, most, cuts=(), kind=jnp.bfloat16):
    values = jax.random.normal(key, dims, jnp.float32) * scale
    if len(cuts) > 0:
        values = block_levels(key, dims, cuts, -0.22, 0.18) * values
    return jnp.clip(values, min=-most, max=most).astype(kind)


def setup_inputs(seed: int = 0, part: int = 0) -> dict:
    seeds = jax.random.split(jax.random.key(seed), 8)
    part_keys = jax.random.split(jax.random.fold_in(seeds[7], part), 8)
    return {
        "observations": noise(part_keys[0], (SLOTS, STATES), 1.0, 6.0, ((0, 16),), jnp.float32),
        "outage_mask": with_ends((jax.random.randint(part_keys[1], (SLOTS, NBLK), 0, 4) < 3).astype(jnp.int32), jax.random.fold_in(part_keys[1], 1), 0, 1),
        "group_length": ragged(part_keys[2], N_TM, N_TM * CAP * 3 // 4, CAP, 1).astype(jnp.int32),
        "prior_mean": noise(part_keys[3], (STATES,), 2.0, 8.0, (), jnp.float32),
        "transition": draw_transition(jax.random.fold_in(seeds[7], 71), part),
        "filter_gain": draw_filter_gain(jax.random.fold_in(seeds[7], 71), part),
        "smoother_gain": draw_smoother_gain(jax.random.fold_in(seeds[7], 71), part),
    }


def reference(observations, outage_mask, group_length, prior_mean, transition, filter_gain, smoother_gain):
    highest = lax.Precision.HIGHEST
    identity_mat = jnp.eye(BLOCK, dtype=jnp.float32)
    updated = jnp.einsum('bij,bjk->bik', identity_mat - filter_gain, transition, precision=highest)
    back_keep = identity_mat - jnp.einsum('bij,bjk->bik', smoother_gain, transition, precision=highest)
    readings = observations.reshape(SLOTS, NBLK, BLOCK)
    position = jnp.arange(SLOTS, dtype=jnp.int32)
    alive_slot = (position % CAP) < group_length[position // CAP]
    observed = (outage_mask == 1) & alive_slot[:, None]
    gain_terms = jnp.einsum('bij,tbj->tbi', filter_gain, readings, precision=highest)

    def forward(state, inputs):
        is_seen, is_alive, gain_term = inputs
        step_mat = jnp.where(is_seen[:, None, None], updated, transition)
        moved_state = jnp.einsum('bij,bj->bi', step_mat, state, precision=highest)
        moved_state = moved_state + jnp.where(is_seen[:, None], gain_term, jnp.float32(0.0))
        moved_state = jnp.where(is_alive, moved_state, state)
        return moved_state, moved_state

    start_state = prior_mean.reshape(NBLK, BLOCK)
    _, filtered = lax.scan(forward, start_state, (observed, alive_slot, gain_terms))

    def backward(carried, inputs):
        later_state, started = carried
        state, is_alive = inputs
        recurred = jnp.einsum('bij,bj->bi', back_keep, state, precision=highest) + jnp.einsum('bij,bj->bi', smoother_gain, later_state, precision=highest)
        result = jnp.where(started, recurred, state)
        next_state = jnp.where(is_alive, result, later_state)
        return (next_state, started | is_alive), jnp.where(is_alive, result, jnp.float32(0.0))

    start_carry = (jnp.zeros((NBLK, BLOCK), jnp.float32), jnp.array(False))
    _, smoothed = lax.scan(backward, start_carry, (filtered, alive_slot), reverse=True)
    return smoothed.reshape(SLOTS, STATES)
```

```python
import functools

import jax
import jax.numpy as jnp
from jax import lax
from jax.experimental import pallas as pl
from jax.experimental.pallas import tpu as pltpu
from jax.sharding import PartitionSpec as P

f32 = jnp.float32
bf16 = jnp.bfloat16
LIMIT_P = 2 * 1024 * 1024
LIMIT_A = 8 * 1024 * 1024
LIMIT_B = 8 * 1024 * 1024


def halves(x):
    high = x.astype(bf16)
    return high, (x - high.astype(f32)).astype(bf16)


def left(x):
    high, low = halves(x)
    return jnp.concatenate([high, low, high], axis=1)


def right(w):
    high, low = halves(w)
    return jnp.concatenate([high, high, low], axis=0)


def dot(a, b):
    return jnp.dot(a, b, preferred_element_type=f32)


def mul(x, w):
    return dot(left(x), right(w))


def side(mats):
    return jnp.concatenate(mats, axis=1)


def below(mats):
    return jnp.concatenate(mats, axis=0)


def pick2(wide, seen, width):
    return jnp.where(seen, wide[:, width:], wide[:, :width])


def pick4(wide, first, second, width):
    return jnp.where(
        first,
        pick2(wide[:, 2 * width :], second, width),
        pick2(wide[:, : 2 * width], second, width),
    )


def shift_levels(live):
    levels = []
    unit = 1
    while unit < live:
        levels.append([unit * m for m in (1, 2, 3) if unit * m < live])
        unit *= 4
    return levels


EXCHANGED = 3


def parity(value, bits):
    total = value & 1
    for k in range(1, bits):
        total = total ^ ((value >> k) & 1)
    return total


def held_block(me, bits, rel, top):
    one = ((me >> 1) & 1) ^ ((rel >> 1) & 1)
    two = ((me >> 2) & 1) ^ ((rel >> 2) & 1)
    low = parity(me, bits) ^ (rel & 1) ^ one ^ two ^ parity(top, 8)
    return low + 2 * one + 4 * two + 8 * top


def pack_kernel(bits, x_hbm, mask_hbm, length_hbm, keep_ref, send_ref, x_ref, mask_ref, length_smem, sems):
    cap, nblocks = mask_ref.shape
    width = keep_ref.shape[1]
    tops = nblocks >> EXCHANGED
    copies = [
        pltpu.make_async_copy(src, dst, sems.at[n])
        for n, (src, dst) in enumerate(((x_hbm, x_ref), (mask_hbm, mask_ref), (length_hbm, length_smem)))
    ]
    for c in copies:
        c.start()
    for c in copies:
        c.wait()
    me = lax.axis_index("tm")
    for rel in range(1 << EXCHANGED):
        target = send_ref if rel & 1 else keep_ref
        for top in range(tops):
            row = ((rel >> 1) * tops + top) * cap
            b = held_block(me, bits, rel, top)
            target[row : row + cap] = x_ref[:, pl.ds(pl.multiple_of(b * width, width), width)]
    marks = mask_ref[...].astype(f32)
    wide = jnp.concatenate([marks] * (width // nblocks), axis=1)
    lane = lax.broadcasted_iota(jnp.int32, (cap, width), 1)
    row = lax.broadcasted_iota(jnp.int32, (cap, width), 0)
    line = jnp.sum(jnp.where(lane // nblocks == row, wide, f32(0.0)), axis=0, keepdims=True)
    meta = jnp.where(row == 0, line, jnp.where(row == 1, length_smem[0].astype(f32), f32(0.0)))
    base = 4 * tops * cap
    keep_ref[base:] = meta
    send_ref[base:] = meta


def in_hbm(*arrays):
    return [pltpu.with_memory_space_constraint(a, pltpu.HBM) for a in arrays]


def in_vmem(*arrays):
    return [pltpu.with_memory_space_constraint(a, pltpu.VMEM) for a in arrays]


def pack(bits, observations, outage_mask, group_length, width):
    cap, nblocks = outage_mask.shape
    rows = nblocks * cap // 2 + 8
    vmem = pl.BlockSpec(memory_space=pltpu.VMEM)
    return pl.pallas_call(
        functools.partial(pack_kernel, bits),
        out_shape=[pltpu.VMEM((rows, width), f32)] * 2,
        in_specs=[pl.BlockSpec(memory_space=pltpu.HBM)] * 2 + [pl.BlockSpec(memory_space=pl.ANY)],
        out_specs=[vmem] * 2,
        scratch_shapes=[
            pltpu.VMEM(observations.shape, f32),
            pltpu.VMEM(outage_mask.shape, jnp.int32),
            pltpu.SMEM((1,), jnp.int32),
            pltpu.SemaphoreType.DMA((3,)),
        ],
        compiler_params=pltpu.CompilerParams(vmem_limit_bytes=LIMIT_P),
        name="pack",
    )(*in_hbm(observations, outage_mask), group_length)


def local(kernel, shapes, name, *arrays):
    vmem = pl.BlockSpec(memory_space=pltpu.VMEM)
    return pl.pallas_call(
        kernel,
        out_shape=[pltpu.VMEM(shape, f32) for shape in shapes],
        in_specs=[vmem] * len(arrays),
        out_specs=[vmem] * len(shapes),
        compiler_params=pltpu.CompilerParams(vmem_limit_bytes=LIMIT_P),
        name=name,
    )(*in_vmem(*arrays))


def deal_kernel(keep_ref, other_ref, *outs):
    half = (outs[0].shape[0] - 8) // 2
    near = 4 * half
    for k, out in enumerate(outs):
        out[:half] = keep_ref[k * half : (k + 1) * half]
        out[half : 2 * half] = other_ref[k * half : (k + 1) * half]
        row = lax.broadcasted_iota(jnp.int32, (8, out.shape[1]), 0)
        shifted = pltpu.roll(other_ref[near : near + 8], 2, 0)
        out[2 * half :] = jnp.where(row < 2, keep_ref[near : near + 8], shifted)


def join_kernel(*refs):
    rows = refs[0].shape[0]
    for n, ref in enumerate(refs[:-1]):
        refs[-1][n * rows : (n + 1) * rows] = ref[...]


def split_kernel(stay_ref, came_ref, *outs):
    half = outs[0].shape[0] // 2
    for k, out in enumerate(outs):
        out[:half] = stay_ref[k * half : (k + 1) * half]
        out[half:] = came_ref[k * half : (k + 1) * half]


def place_kernel(bits, *refs):
    out_ref = refs[-1]
    cap = out_ref.shape[0]
    width = refs[0].shape[1]
    tops = refs[0].shape[0] // (2 * cap)
    me = lax.axis_index("tm")
    for rel in range(1 << EXCHANGED):
        for top in range(tops):
            row = ((rel & 1) * tops + top) * cap
            b = held_block(me, bits, rel, top)
            out_ref[:, pl.ds(pl.multiple_of(b * width, width), width)] = refs[rel >> 1][row : row + cap]


def place(bits, shape, *arrays):
    vmem = pl.BlockSpec(memory_space=pltpu.VMEM)
    return pl.pallas_call(
        functools.partial(place_kernel, bits),
        out_shape=jax.ShapeDtypeStruct(shape, f32),
        in_specs=[vmem] * len(arrays),
        out_specs=vmem,
        compiler_params=pltpu.CompilerParams(vmem_limit_bytes=LIMIT_P),
        name="place",
    )(*in_vmem(*arrays))


def model_kernel(
    blocks_of,
    live,
    t_hbm,
    k_hbm,
    s_hbm,
    gain_ref,
    step_ref,
    pair_ref,
    rowprod_ref,
    colprod_ref,
    back_ref,
    power_ref,
    t_ref,
    k_ref,
    s_ref,
    sems,
):
    nb, width = t_ref.shape[0], t_ref.shape[1]
    levels = shift_levels(live)
    copies = []
    for j, b in enumerate(blocks_of()):
        for n, (src, dst) in enumerate(((t_hbm, t_ref), (k_hbm, k_ref), (s_hbm, s_ref))):
            copies.append(pltpu.make_async_copy(src.at[b], dst.at[j], sems.at[j, n]))
    for c in copies:
        c.start()
    for c in copies:
        c.wait()
    eye = (
        lax.broadcasted_iota(jnp.int32, (width, width), 0)
        == lax.broadcasted_iota(jnp.int32, (width, width), 1)
    ).astype(f32)

    for j in range(nb):
        t = t_ref[j]
        k = k_ref[j]
        rt = t.T
        rg = s_ref[j].T
        gain_ref[j] = right(k)
        ru = rt - dot(left(rt), gain_ref[j])
        u = t - mul(k, t)
        step_ref[j] = right(side([rt, ru]))
        row2 = dot(left(below([rt, ru])), step_ref[j])
        row2 = [row2[a * width : (a + 1) * width, b * width : (b + 1) * width] for a in (0, 1) for b in (0, 1)]
        col2 = mul(below([t, u]), side([t, u]))
        col2 = [col2[b * width : (b + 1) * width, a * width : (a + 1) * width] for a in (0, 1) for b in (0, 1)]
        pair_ref[j] = right(side(row2))
        row4 = dot(left(below(row2)), pair_ref[j])
        col4 = mul(below(col2), side(col2))
        for p in range(4):
            for q in range(4):
                rowprod_ref[j, 4 * p + q] = row4[p * width : (p + 1) * width, q * width : (q + 1) * width]
                colprod_ref[j, 4 * p + q] = col4[q * width : (q + 1) * width, p * width : (p + 1) * width]
        back_ref[j] = right(eye - mul(rt, rg))
        power = rg
        for n, level in enumerate(levels):
            rights = [right(power)]
            if len(level) > 1:
                second = dot(left(power), rights[0])
                rights.append(right(second))
                both = dot(left(second), side(rights))
                rights.append(right(both[:, :width]))
                power = both[:, width:]
            for m in range(len(level)):
                power_ref[j, n, m * 3 * width : (m + 1) * 3 * width] = rights[m]


def prepare(blocks_of, nb, live, transition, filter_gain, smoother_gain):
    width = transition.shape[1]
    levels = shift_levels(live)
    hbm = pl.BlockSpec(memory_space=pltpu.HBM)
    vmem = pl.BlockSpec(memory_space=pltpu.VMEM)
    return pl.pallas_call(
        functools.partial(model_kernel, blocks_of, live),
        out_shape=[
            pltpu.VMEM((nb, 3 * width, width), bf16),
            pltpu.VMEM((nb, 3 * width, 2 * width), bf16),
            pltpu.VMEM((nb, 3 * width, 4 * width), bf16),
            pltpu.VMEM((nb, 16, width, width), f32),
            pltpu.VMEM((nb, 16, width, width), f32),
            pltpu.VMEM((nb, 3 * width, width), bf16),
            pltpu.VMEM((nb, len(levels), 9 * width, width), bf16),
        ],
        in_specs=[hbm] * 3,
        out_specs=[vmem] * 7,
        scratch_shapes=[
            pltpu.VMEM((nb, width, width), f32),
            pltpu.VMEM((nb, width, width), f32),
            pltpu.VMEM((nb, width, width), f32),
            pltpu.SemaphoreType.DMA((nb, 3)),
        ],
        compiler_params=pltpu.CompilerParams(vmem_limit_bytes=LIMIT_A),
        cost_estimate=pl.CostEstimate(flops=10**9, bytes_accessed=4 * 10**6, transcendentals=0),
        name="prepare",
    )(*in_hbm(transition, filter_gain, smoother_gain))


def smoother_kernel(
    bits,
    blocks_of,
    live,
    held_ref,
    arrived_ref,
    prior_ref,
    k_ref,
    step_ref,
    pair_ref,
    rowprod_ref,
    colprod_ref,
    back_ref,
    power_ref,
    stay_ref,
    leave_ref,
    gain_ref,
    seen_ref,
    col_ref,
    colgain_ref,
    start_ref,
    filt_ref,
    bits_smem,
    starts_smem,
    y_ref,
    meta_ref,
    meta_smem,
    meta_sem,
):
    nb, width = gain_ref.shape[0], y_ref.shape[2]
    nblocks = prior_ref.shape[0]
    groups = 2 * y_ref.shape[0]
    cap = stay_ref.shape[0] // (4 * nb)
    meta_row = 2 * nb * cap
    nchunks = live // 4
    levels = shift_levels(live)
    blocks = blocks_of()
    me = lax.axis_index("tm")

    count = held_ref.shape[0]
    y_ref[:count] = held_ref[...]
    y_ref[count:] = arrived_ref[...]
    meta_ref[...] = y_ref[:, meta_row:].astype(jnp.int32)
    fetch = pltpu.make_async_copy(meta_ref, meta_smem, meta_sem)
    fetch.start()
    fetch.wait()

    places = [((me ^ g) >> 1, parity(me ^ g, bits)) for g in range(groups)]
    starts = [0]
    for g in range(groups):
        starts_smem[g] = starts[g]
        starts.append(starts[-1] + meta_smem[places[g][0], 2 * places[g][1] + 1, 0])
    for j, b in enumerate(blocks):
        for g in range(groups):
            for s in range(cap):
                bits_smem[j, starts[g] + s] = meta_smem[places[g][0], 2 * places[g][1], s * nblocks + b]

    ones = jnp.ones((width, width), bf16)
    lanes = lax.broadcasted_iota(jnp.int32, (cap, width), 1)
    rows = lax.broadcasted_iota(jnp.int32, (cap, width), 0)
    for j, b in enumerate(blocks):
        readings = below(
            [y_ref[pk, pl.ds(pl.multiple_of((near * nb + j) * cap, cap), cap), :] for pk, near in places]
        )
        gains = dot(left(readings), k_ref[j])
        chosen = lanes == rows * nblocks + b
        marks = below(
            [
                jnp.where(
                    chosen,
                    jnp.broadcast_to(y_ref[pk, pl.ds(meta_row + 2 * near, 1), :], (cap, width)),
                    f32(0.0),
                )
                for pk, near in places
            ]
        )
        seen = dot(marks.astype(bf16), ones)
        gains = jnp.where(seen > 0.5, gains, f32(0.0))
        for g in range(groups):
            gain_ref[j, pl.ds(starts[g], cap), :] = gains[g * cap : (g + 1) * cap]
            seen_ref[j, pl.ds(starts[g], cap), :] = seen[g * cap : (g + 1) * cap]

    gain = [[gain_ref[j, pl.ds(s, nchunks, stride=4), :] for s in range(4)] for j in range(nb)]
    seen = [[seen_ref[j, pl.ds(s, nchunks, stride=4), :] > 0.5 for s in range(4)] for j in range(nb)]
    twos = []
    for j in range(nb):
        first = pick2(dot(left(gain[j][0]), step_ref[j]), seen[j][1], width) + gain[j][1]
        last = pick2(dot(left(gain[j][2]), step_ref[j]), seen[j][3], width) + gain[j][3]
        four = pick4(dot(left(first), pair_ref[j]), seen[j][2], seen[j][3], width) + last
        twos.append(first)
        filt_ref[j, :nchunks] = four
        pad = -nchunks % width
        padded = below([four, jnp.zeros((pad, width), f32)]) if pad else four
        for n in range(padded.shape[0] // width):
            colgain_ref[j, n] = padded[n * width : (n + 1) * width].T
        start_ref[j, pl.ds(0, 1), :] = prior_ref[pl.ds(blocks[j], 1), :]

    lane_full = lax.broadcasted_iota(jnp.int32, (width, width), 1)

    def pattern(j, c):
        o = [bits_smem[j, 4 * c + s] for s in range(4)]
        return ((o[0] * 2 + o[1]) * 2 + o[2]) * 2 + o[3]

    def two_steps(i, state):
        moved = []
        c = 2 * i
        part = c // width
        lane = c - part * width
        here = lane_full == lane
        for j in range(nb):
            prod = colprod_ref[j, pattern(j, c)] * state[j]
            prod = prod + jnp.where(here, colgain_ref[j, part], f32(0.0))
            column = jnp.broadcast_to(jnp.sum(prod, axis=1, keepdims=True), (width, width))
            pltpu.store(col_ref.at[j, part], column, mask=here)
            row = jnp.sum(rowprod_ref[j, pattern(j, c + 1)] * column, axis=0, keepdims=True)
            row = row + filt_ref[j, pl.ds(c + 1, 1), :]
            start_ref[j, pl.ds(c + 2, 1), :] = row
            moved.append(row)
        return tuple(moved)

    lax.fori_loop(0, nchunks // 2, two_steps, tuple(prior_ref[pl.ds(b, 1), :] for b in blocks))

    for j in range(nb):
        for n in range(col_ref.shape[1]):
            count = min(width, nchunks - n * width) // 2
            flipped = col_ref[j, n].T
            col_ref[j, n] = flipped
            start_ref[j, pl.ds(n * width + 1, count, stride=2), :] = col_ref[j, n, pl.ds(0, count, stride=2), :]
        begin = start_ref[j, :nchunks]
        lefts = left(begin)
        one = pick2(dot(lefts, step_ref[j]), seen[j][0], width) + gain[j][0]
        two = pick4(dot(lefts, pair_ref[j]), seen[j][0], seen[j][1], width) + twos[j]
        three = pick2(dot(left(two), step_ref[j]), seen[j][2], width) + gain[j][2]
        four = start_ref[j, 1 : nchunks + 1]
        for s, value in enumerate((one, two, three, four)):
            filt_ref[j, pl.ds(s, nchunks, stride=4), :] = value
    for j in range(nb):
        tail = filt_ref.shape[1] - live
        filtered = filt_ref[j, :live]
        smoothed = dot(left(filtered), back_ref[j])
        is_last = lax.broadcasted_iota(jnp.int32, (live, width), 0) == live - 1
        smoothed = jnp.where(is_last, filtered, smoothed)
        filt_ref[j, live:] = jnp.zeros((tail, width), f32)
        for n, level in enumerate(levels):
            filt_ref[j, :live] = smoothed
            moved = side([left(filt_ref[j, sh : sh + live]) for sh in level])
            smoothed = smoothed + dot(moved, power_ref[j, n, : 3 * width * len(level)])
        filt_ref[j, :live] = smoothed
        for d in range(1 << EXCHANGED):
            near = parity(d, EXCHANGED)
            value = filt_ref[j, pl.ds(starts_smem[me ^ d], cap), :]
            value = jnp.where(rows < meta_smem[d >> 1, 2 * near + 1, 0], value, f32(0.0))
            row = ((d >> 1) * nb + j) * cap
            (leave_ref if near else stay_ref)[row : row + cap] = value


def smooth(bits, blocks_of, nb, cap, live, held, arrived, prior, model):
    packages = 2 * held.shape[0]
    rows, width = held.shape[1:]
    nchunks = live // 4
    levels = shift_levels(live)
    parts = -(-nchunks // width)
    vmem = pl.BlockSpec(memory_space=pltpu.VMEM)
    tail = max(max(level) for level in levels) + cap
    return pl.pallas_call(
        functools.partial(smoother_kernel, bits, blocks_of, live),
        out_shape=[pltpu.VMEM((4 * nb * cap, width), f32)] * 2,
        in_specs=[vmem] * 10,
        out_specs=[vmem] * 2,
        scratch_shapes=[
            pltpu.VMEM((nb, live + cap, width), f32),
            pltpu.VMEM((nb, live + cap, width), f32),
            pltpu.VMEM((nb, parts, width, width), f32),
            pltpu.VMEM((nb, parts, width, width), f32),
            pltpu.VMEM((nb, nchunks + cap, width), f32),
            pltpu.VMEM((nb, live + tail, width), f32),
            pltpu.SMEM((nb, live + cap), jnp.int32),
            pltpu.SMEM((2 * packages,), jnp.int32),
            pltpu.VMEM((packages, rows, width), f32),
            pltpu.VMEM((packages, 8, width), jnp.int32),
            pltpu.SMEM((packages, 8, width), jnp.int32),
            pltpu.SemaphoreType.DMA,
        ],
        compiler_params=pltpu.CompilerParams(vmem_limit_bytes=LIMIT_B),
        name="smooth",
    )(*in_vmem(held, arrived), prior, *in_vmem(*model))


def permuted(x, mask):
    count = lax.axis_size("tm")
    return lax.ppermute(x, "tm", [(i, i ^ mask) for i in range(count)])


def shards(observations, outage_mask, group_length, prior_mean, transition, filter_gain, smoother_gain):
    cap = observations.shape[0]
    nblocks, width = transition.shape[0], transition.shape[1]
    bits = lax.axis_size("tm").bit_length() - 1
    nb = nblocks >> EXCHANGED
    live = (cap << bits) * 3 // 4
    half = nb * cap

    def blocks_of():
        return [held_block(lax.axis_index("tm"), bits, 0, top) for top in range(nb)]

    masks = (3, 5, 6)
    model = prepare(blocks_of, nb, live, transition, filter_gain, smoother_gain)
    keep, send = pack(bits, observations, outage_mask, group_length, width)
    package = (2 * half + 8, width)
    dealt = local(deal_kernel, [package] * 4, "deal", keep, permuted(send, 1))
    crossed = [permuted(p, mask) for p, mask in zip(dealt[1:], masks)]
    (held,) = local(join_kernel, [(4 * package[0], width)], "join", dealt[0], *crossed)
    held = held.reshape(4, *package)
    arrived = permuted(held, (1 << EXCHANGED) | 1)
    for k in range(EXCHANGED + 1, bits):
        held = jnp.concatenate([held, arrived])
        arrived = permuted(held, (1 << k) | 1)
    stay, leave = smooth(bits, blocks_of, nb, cap, live, held, arrived, prior_mean.reshape(nblocks, width), model)
    split = local(split_kernel, [(2 * half, width)] * 4, "split", stay, permuted(leave, 1))
    crossed = [permuted(p, mask) for p, mask in zip(split[1:], masks)]
    return place(bits, observations.shape, split[0], *crossed)


def solution(mesh):
    placed = (
        P(("parts", "tm"), None),
        P(("parts", "tm"), None),
        P(("parts", "tm")),
        P("parts"),
        P(),
        P(),
        P(),
    )
    return jax.shard_map(
        shards, mesh=mesh, in_specs=placed, out_specs=P(("parts", "tm"), None), check_vma=False
    )
```

```python
import functools

import jax
import jax.numpy as jnp
from jax import lax
from jax.experimental import pallas as pl
from jax.experimental.pallas import tpu as pltpu
from jax.sharding import PartitionSpec as P

f32 = jnp.float32
bf16 = jnp.bfloat16
LIMIT_P = 2 * 1024 * 1024
LIMIT_A = 8 * 1024 * 1024
LIMIT_B = 8 * 1024 * 1024


def halves(x):
    high = x.astype(bf16)
    return high, (x - high.astype(f32)).astype(bf16)


def left(x):
    high, low = halves(x)
    return jnp.concatenate([high, low, high], axis=1)


def right(w):
    high, low = halves(w)
    return jnp.concatenate([high, high, low], axis=0)


def dot(a, b):
    return jnp.dot(a, b, preferred_element_type=f32)


def mul(x, w):
    return dot(left(x), right(w))


def side(mats):
    return jnp.concatenate(mats, axis=1)


def below(mats):
    return jnp.concatenate(mats, axis=0)


def pick2(wide, seen, width):
    return jnp.where(seen, wide[:, width:], wide[:, :width])


def pick4(wide, first, second, width):
    return jnp.where(
        first,
        pick2(wide[:, 2 * width :], second, width),
        pick2(wide[:, : 2 * width], second, width),
    )


def shift_levels(live):
    levels = []
    unit = 1
    while unit < live:
        levels.append([unit * m for m in (1, 2, 3) if unit * m < live])
        unit *= 4
    return levels


EXCHANGED = 3


def parity(value, bits):
    total = value & 1
    for k in range(1, bits):
        total = total ^ ((value >> k) & 1)
    return total


def held_block(me, bits, rel, top):
    one = ((me >> 1) & 1) ^ ((rel >> 1) & 1)
    two = ((me >> 2) & 1) ^ ((rel >> 2) & 1)
    low = parity(me, bits) ^ (rel & 1) ^ one ^ two ^ parity(top, 8)
    return low + 2 * one + 4 * two + 8 * top


def pack_kernel(bits, x_hbm, mask_hbm, length_hbm, keep_ref, send_ref, x_ref, mask_ref, length_smem, sems):
    cap, nblocks = mask_ref.shape
    width = keep_ref.shape[1]
    tops = nblocks >> EXCHANGED
    copies = [
        pltpu.make_async_copy(src, dst, sems.at[n])
        for n, (src, dst) in enumerate(((x_hbm, x_ref), (mask_hbm, mask_ref), (length_hbm, length_smem)))
    ]
    for c in copies:
        c.start()
    for c in copies:
        c.wait()
    me = lax.axis_index("tm")
    for rel in range(1 << EXCHANGED):
        target = send_ref if rel & 1 else keep_ref
        for top in range(tops):
            row = ((rel >> 1) * tops + top) * cap
            b = held_block(me, bits, rel, top)
            target[row : row + cap] = x_ref[:, pl.ds(pl.multiple_of(b * width, width), width)]
    marks = mask_ref[...].astype(f32)
    wide = jnp.concatenate([marks] * (width // nblocks), axis=1)
    lane = lax.broadcasted_iota(jnp.int32, (cap, width), 1)
    row = lax.broadcasted_iota(jnp.int32, (cap, width), 0)
    line = jnp.sum(jnp.where(lane // nblocks == row, wide, f32(0.0)), axis=0, keepdims=True)
    meta = jnp.where(row == 0, line, jnp.where(row == 1, length_smem[0].astype(f32), f32(0.0)))
    base = 4 * tops * cap
    keep_ref[base:] = meta
    send_ref[base:] = meta


def in_hbm(*arrays):
    return [pltpu.with_memory_space_constraint(a, pltpu.HBM) for a in arrays]


def in_vmem(*arrays):
    return [pltpu.with_memory_space_constraint(a, pltpu.VMEM) for a in arrays]


def pack(bits, observations, outage_mask, group_length, width):
    cap, nblocks = outage_mask.shape
    rows = nblocks * cap // 2 + 8
    vmem = pl.BlockSpec(memory_space=pltpu.VMEM)
    return pl.pallas_call(
        functools.partial(pack_kernel, bits),
        out_shape=[pltpu.VMEM((rows, width), f32)] * 2,
        in_specs=[pl.BlockSpec(memory_space=pltpu.HBM)] * 2 + [pl.BlockSpec(memory_space=pl.ANY)],
        out_specs=[vmem] * 2,
        scratch_shapes=[
            pltpu.VMEM(observations.shape, f32),
            pltpu.VMEM(outage_mask.shape, jnp.int32),
            pltpu.SMEM((1,), jnp.int32),
            pltpu.SemaphoreType.DMA((3,)),
        ],
        compiler_params=pltpu.CompilerParams(vmem_limit_bytes=LIMIT_P),
        name="pack",
    )(*in_hbm(observations, outage_mask), group_length)


def local(kernel, shapes, name, *arrays):
    vmem = pl.BlockSpec(memory_space=pltpu.VMEM)
    return pl.pallas_call(
        kernel,
        out_shape=[pltpu.VMEM(shape, f32) for shape in shapes],
        in_specs=[vmem if a.dtype == f32 else pl.BlockSpec(memory_space=pl.ANY) for a in arrays],
        out_specs=[vmem] * len(shapes),
        compiler_params=pltpu.CompilerParams(vmem_limit_bytes=LIMIT_P),
        name=name,
    )(*in_vmem(*arrays))


def deal_kernel(keep_ref, other_ref, *outs):
    half = (outs[0].shape[0] - 8) // 2
    near = 4 * half
    for k, out in enumerate(outs):
        out[:half] = keep_ref[k * half : (k + 1) * half]
        out[half : 2 * half] = other_ref[k * half : (k + 1) * half]
        row = lax.broadcasted_iota(jnp.int32, (8, out.shape[1]), 0)
        shifted = pltpu.roll(other_ref[near : near + 8], 2, 0)
        out[2 * half :] = jnp.where(row < 2, keep_ref[near : near + 8], shifted)


def join_kernel(_, *refs):
    out_ref = refs[-1]
    rows = refs[0].shape[0] - 8
    for k, ref in enumerate(refs[:-1]):
        out_ref[k * rows : (k + 1) * rows] = ref[:rows]
        out_ref[4 * rows + 4 * k : 4 * rows + 4 * k + 4] = ref[rows : rows + 4]


def split_kernel(stay_ref, came_ref, *outs):
    half = outs[0].shape[0] // 2
    for k, out in enumerate(outs):
        out[:half] = stay_ref[k * half : (k + 1) * half]
        out[half:] = came_ref[k * half : (k + 1) * half]


def place_kernel(bits, *refs):
    out_ref = refs[-1]
    cap = out_ref.shape[0]
    width = refs[0].shape[1]
    tops = refs[0].shape[0] // (2 * cap)
    me = lax.axis_index("tm")
    for rel in range(1 << EXCHANGED):
        for top in range(tops):
            row = ((rel & 1) * tops + top) * cap
            b = held_block(me, bits, rel, top)
            out_ref[:, pl.ds(pl.multiple_of(b * width, width), width)] = refs[rel >> 1][row : row + cap]


def place(bits, shape, *arrays):
    vmem = pl.BlockSpec(memory_space=pltpu.VMEM)
    return pl.pallas_call(
        functools.partial(place_kernel, bits),
        out_shape=jax.ShapeDtypeStruct(shape, f32),
        in_specs=[vmem] * len(arrays),
        out_specs=vmem,
        compiler_params=pltpu.CompilerParams(vmem_limit_bytes=LIMIT_P),
        name="place",
    )(*in_vmem(*arrays))


def model_kernel(
    blocks_of,
    t_hbm,
    k_hbm,
    s_hbm,
    after_ref,
    gain_ref,
    step_ref,
    pair_ref,
    back_ref,
    row_ref,
    col_ref,
    power_ref,
    t_ref,
    k_ref,
    s_ref,
    sems,
):
    nb, width = t_ref.shape[0], t_ref.shape[1]
    copies = []
    for j, b in enumerate(blocks_of()):
        for n, (src, dst) in enumerate(((t_hbm, t_ref), (k_hbm, k_ref), (s_hbm, s_ref))):
            copies.append(pltpu.make_async_copy(src.at[b], dst.at[j], sems.at[j, n]))
    for c in copies:
        c.start()
    for c in copies:
        c.wait()
    eye = (
        lax.broadcasted_iota(jnp.int32, (width, width), 0)
        == lax.broadcasted_iota(jnp.int32, (width, width), 1)
    ).astype(f32)
    both = range(nb)
    rt = [t_ref[j].T for j in both]
    for j in both:
        power_ref[j] = s_ref[j].T
        gain_ref[j] = right(k_ref[j])
    ru = [rt[j] - dot(left(rt[j]), gain_ref[j]) for j in both]
    u = [t_ref[j] - mul(k_ref[j], t_ref[j]) for j in both]
    for j in both:
        step_ref[j] = right(side([rt[j], ru[j]]))
    row2 = [dot(left(below([rt[j], ru[j]])), step_ref[j]) for j in both]
    col2 = [mul(below([t_ref[j], u[j]]), side([t_ref[j], u[j]])) for j in both]
    for j in both:
        back_ref[j] = right(eye - mul(rt[j], power_ref[j]))
        for a in (0, 1):
            for b in (0, 1):
                one, two = slice(a * width, (a + 1) * width), slice(b * width, (b + 1) * width)
                row_ref[j, (2 * a + b) * width : (2 * a + b + 1) * width] = row2[j][one, two]
                col_ref[j, (2 * a + b) * width : (2 * a + b + 1) * width] = col2[j][two, one]
        pair_ref[j] = right(side([row_ref[j, n * width : (n + 1) * width] for n in range(4)]))


def product_kernel(live, pair_ref, row_ref, col_ref, gain_ref, after_ref, rowprod_ref, colprod_ref, power_ref):
    nb, _, width = row_ref.shape
    levels = shift_levels(live)
    both = range(nb)
    power = [gain_ref[j] for j in both]
    for j in both:
        row4 = dot(left(row_ref[j]), pair_ref[j])
        col4 = mul(col_ref[j], side([col_ref[j, n * width : (n + 1) * width] for n in range(4)]))
        for p in range(4):
            for q in range(4):
                rowprod_ref[j, 4 * p + q] = row4[p * width : (p + 1) * width, q * width : (q + 1) * width]
                colprod_ref[j, 4 * p + q] = col4[q * width : (q + 1) * width, p * width : (p + 1) * width]
    for n, level in enumerate(levels):
        rights = [[right(power[j])] for j in both]
        if len(level) > 1:
            second = [dot(left(power[j]), rights[j][0]) for j in both]
            for j in both:
                rights[j].append(right(second[j]))
            double = [dot(left(second[j]), side(rights[j])) for j in both]
            for j in both:
                rights[j].append(right(double[j][:, :width]))
                power[j] = double[j][:, width:]
        for j in both:
            for m in range(len(level)):
                power_ref[j, n, m * 3 * width : (m + 1) * 3 * width] = rights[j][m]


def prepare(blocks_of, nb, transition, filter_gain, smoother_gain, after):
    width = transition.shape[1]
    hbm = pl.BlockSpec(memory_space=pltpu.HBM)
    vmem = pl.BlockSpec(memory_space=pltpu.VMEM)
    return pl.pallas_call(
        functools.partial(model_kernel, blocks_of),
        out_shape=[
            pltpu.VMEM((nb, 3 * width, width), bf16),
            pltpu.VMEM((nb, 3 * width, 2 * width), bf16),
            pltpu.VMEM((nb, 3 * width, 4 * width), bf16),
            pltpu.VMEM((nb, 3 * width, width), bf16),
            pltpu.VMEM((nb, 4 * width, width), f32),
            pltpu.VMEM((nb, 4 * width, width), f32),
            pltpu.VMEM((nb, width, width), f32),
        ],
        in_specs=[hbm] * 3 + [pl.BlockSpec(memory_space=pl.ANY)],
        out_specs=[vmem] * 7,
        scratch_shapes=[
            pltpu.VMEM((nb, width, width), f32),
            pltpu.VMEM((nb, width, width), f32),
            pltpu.VMEM((nb, width, width), f32),
            pltpu.SemaphoreType.DMA((nb, 3)),
        ],
        compiler_params=pltpu.CompilerParams(vmem_limit_bytes=LIMIT_A),
        cost_estimate=pl.CostEstimate(flops=10**9, bytes_accessed=4 * 10**6, transcendentals=0),
        name="prepare",
    )(*in_hbm(transition, filter_gain, smoother_gain), after)


def products(live, pair, row2, col2, gain, after):
    nb, _, width = row2.shape
    levels = shift_levels(live)
    vmem = pl.BlockSpec(memory_space=pltpu.VMEM)
    return pl.pallas_call(
        functools.partial(product_kernel, live),
        out_shape=[
            pltpu.VMEM((nb, 16, width, width), f32),
            pltpu.VMEM((nb, 16, width, width), f32),
            pltpu.VMEM((nb, len(levels), 9 * width, width), bf16),
        ],
        in_specs=[vmem] * 4 + [pl.BlockSpec(memory_space=pl.ANY)],
        out_specs=[vmem] * 3,
        compiler_params=pltpu.CompilerParams(vmem_limit_bytes=LIMIT_A),
        cost_estimate=pl.CostEstimate(flops=10**9, bytes_accessed=4 * 10**6, transcendentals=0),
        name="products",
    )(*in_vmem(pair, row2, col2, gain), after)


def smoother_kernel(
    bits,
    blocks_of,
    live,
    held_ref,
    arrived_ref,
    prior_ref,
    k_ref,
    step_ref,
    pair_ref,
    rowprod_ref,
    colprod_ref,
    back_ref,
    power_ref,
    stay_ref,
    leave_ref,
    gain_ref,
    seen_ref,
    col_ref,
    colgain_ref,
    start_ref,
    filt_ref,
    starts_smem,
    y_ref,
    meta_ref,
    meta_smem,
    order_ref,
    order_smem,
    sems,
):
    nb, width = gain_ref.shape[0], y_ref.shape[2]
    nblocks = prior_ref.shape[0]
    groups = 8 * y_ref.shape[0]
    cap = stay_ref.shape[0] // (4 * nb)
    meta_row = 8 * nb * cap
    nchunks = live // 4
    levels = shift_levels(live)
    blocks = blocks_of()
    me = lax.axis_index("tm")
    odd = parity(me, bits)

    count = held_ref.shape[0]
    meta_ref[:count] = held_ref[:, meta_row:].astype(jnp.int32)
    meta_ref[count:] = arrived_ref[:, meta_row:].astype(jnp.int32)
    fetch = pltpu.make_async_copy(meta_ref, meta_smem, sems.at[0])
    fetch.start()
    y_ref[:count] = held_ref[...]
    y_ref[count:] = arrived_ref[...]
    places = []
    for g in range(groups):
        d = me ^ g
        places.append((d >> 3, (d >> 1) & 3, odd ^ parity(g, bits)))

    ones = jnp.ones((width, width), bf16)
    lanes = lax.broadcasted_iota(jnp.int32, (cap, width), 1)
    rows = lax.broadcasted_iota(jnp.int32, (cap, width), 0)
    packed = []
    for j, b in enumerate(blocks):
        readings = below(
            [
                y_ref[top, pl.ds(pl.multiple_of(((k * 2 + near) * nb + j) * cap, cap), cap), :]
                for top, k, near in places
            ]
        )
        gains = dot(left(readings), k_ref[j])
        chosen = lanes == rows * nblocks + b
        marks = below(
            [
                jnp.where(
                    chosen,
                    jnp.broadcast_to(y_ref[top, pl.ds(meta_row + 4 * k + 2 * near, 1), :], (cap, width)),
                    f32(0.0),
                )
                for top, k, near in places
            ]
        )
        seen = dot(marks.astype(bf16), ones)
        gains = jnp.where(seen > 0.5, gains, f32(0.0))
        packed.append((gains, seen))
    fetch.wait()
    starts = [0]
    for g in range(groups):
        top, k, near = places[g]
        starts_smem[g] = starts[g]
        starts.append(starts[-1] + meta_smem[top, 4 * k + 2 * near + 1, 0])
    for j, (gains, seen) in enumerate(packed):
        for g in range(groups):
            gain_ref[j, pl.ds(starts[g], cap), :] = gains[g * cap : (g + 1) * cap]
            seen_ref[j, pl.ds(starts[g], cap), :] = seen[g * cap : (g + 1) * cap]

    gain = [[gain_ref[j, pl.ds(s, nchunks, stride=4), :] for s in range(4)] for j in range(nb)]
    marks = [[seen_ref[j, pl.ds(s, nchunks, stride=4), :] for s in range(4)] for j in range(nb)]
    for j in range(nb):
        order = ((marks[j][0] * 2.0 + marks[j][1]) * 2.0 + marks[j][2]) * 2.0 + marks[j][3]
        order_ref[j] = order.astype(jnp.int32)
    fetch = pltpu.make_async_copy(order_ref, order_smem, sems.at[1])
    fetch.start()
    seen = [[m > 0.5 for m in marks[j]] for j in range(nb)]
    begun = [
        dot(left(below([gain[j][0], gain[j][2]])), step_ref[j]) for j in range(nb)
    ]
    twos, lasts, fours = [], [], []
    for j in range(nb):
        twos.append(pick2(begun[j][:nchunks], seen[j][1], width) + gain[j][1])
        lasts.append(pick2(begun[j][nchunks:], seen[j][3], width) + gain[j][3])
    wide = [dot(left(twos[j]), pair_ref[j]) for j in range(nb)]
    for j in range(nb):
        four = pick4(wide[j], seen[j][2], seen[j][3], width) + lasts[j]
        filt_ref[j, :nchunks] = four
        pad = -nchunks % width
        padded = below([four, jnp.zeros((pad, width), f32)]) if pad else four
        for n in range(padded.shape[0] // width):
            colgain_ref[j, n] = padded[n * width : (n + 1) * width].T
        start_ref[j, pl.ds(0, 1), :] = prior_ref[pl.ds(blocks[j], 1), :]
    fetch.wait()

    lane_full = lax.broadcasted_iota(jnp.int32, (width, width), 1)

    def pattern(j, c):
        return order_smem[j, c, 0]

    def two_steps(i, state):
        moved = []
        c = 2 * i
        part = c // width
        lane = c - part * width
        here = lane_full == lane
        for j in range(nb):
            prod = colprod_ref[j, pattern(j, c)] * state[j]
            prod = prod + jnp.where(here, colgain_ref[j, part], f32(0.0))
            column = jnp.broadcast_to(jnp.sum(prod, axis=1, keepdims=True), (width, width))
            pltpu.store(col_ref.at[j, part], column, mask=here)
            row = jnp.sum(rowprod_ref[j, pattern(j, c + 1)] * column, axis=0, keepdims=True)
            row = row + filt_ref[j, pl.ds(c + 1, 1), :]
            start_ref[j, pl.ds(c + 2, 1), :] = row
            moved.append(row)
        return tuple(moved)

    lax.fori_loop(0, nchunks // 2, two_steps, tuple(prior_ref[pl.ds(b, 1), :] for b in blocks))

    for j in range(nb):
        for n in range(col_ref.shape[1]):
            count = min(width, nchunks - n * width) // 2
            flipped = col_ref[j, n].T
            col_ref[j, n] = flipped
            start_ref[j, pl.ds(n * width + 1, count, stride=2), :] = col_ref[j, n, pl.ds(0, count, stride=2), :]
    lefts = [left(start_ref[j, :nchunks]) for j in range(nb)]
    ones = [dot(lefts[j], step_ref[j]) for j in range(nb)]
    pairs = [dot(lefts[j], pair_ref[j]) for j in range(nb)]
    pairs = [pick4(pairs[j], seen[j][0], seen[j][1], width) + twos[j] for j in range(nb)]
    threes = [dot(left(pairs[j]), step_ref[j]) for j in range(nb)]
    for j in range(nb):
        one = pick2(ones[j], seen[j][0], width) + gain[j][0]
        three = pick2(threes[j], seen[j][2], width) + gain[j][2]
        four = start_ref[j, 1 : nchunks + 1]
        for s, value in enumerate((one, pairs[j], three, four)):
            filt_ref[j, pl.ds(s, nchunks, stride=4), :] = value
    is_last = lax.broadcasted_iota(jnp.int32, (live, width), 0) == live - 1
    tail = filt_ref.shape[1] - live
    filtered = [filt_ref[j, :live] for j in range(nb)]
    smoothed = [jnp.where(is_last, x, dot(left(x), back_ref[j])) for j, x in enumerate(filtered)]
    for j in range(nb):
        filt_ref[j, live:] = jnp.zeros((tail, width), f32)
    for n, level in enumerate(levels):
        for j in range(nb):
            filt_ref[j, :live] = smoothed[j]
        for j in range(nb):
            moved = side([left(filt_ref[j, sh : sh + live]) for sh in level])
            smoothed[j] = smoothed[j] + dot(moved, power_ref[j, n, : 3 * width * len(level)])
    for j in range(nb):
        filt_ref[j, :live] = smoothed[j]
    for j in range(nb):
        for d in range(1 << EXCHANGED):
            near = parity(d, EXCHANGED)
            value = filt_ref[j, pl.ds(starts_smem[me ^ d], cap), :]
            value = jnp.where(rows < meta_smem[0, 4 * (d >> 1) + 2 * near + 1, 0], value, f32(0.0))
            row = ((d >> 1) * nb + j) * cap
            (leave_ref if near else stay_ref)[row : row + cap] = value


def smooth(bits, blocks_of, nb, cap, live, held, arrived, prior, model):
    tops = 2 * held.shape[0]
    rows, width = held.shape[1:]
    nchunks = live // 4
    levels = shift_levels(live)
    parts = -(-nchunks // width)
    vmem = pl.BlockSpec(memory_space=pltpu.VMEM)
    tail = max(max(level) for level in levels) + cap
    return pl.pallas_call(
        functools.partial(smoother_kernel, bits, blocks_of, live),
        out_shape=[pltpu.VMEM((4 * nb * cap, width), f32)] * 2,
        in_specs=[vmem] * 10,
        out_specs=[vmem] * 2,
        scratch_shapes=[
            pltpu.VMEM((nb, live + cap, width), f32),
            pltpu.VMEM((nb, live + cap, width), f32),
            pltpu.VMEM((nb, parts, width, width), f32),
            pltpu.VMEM((nb, parts, width, width), f32),
            pltpu.VMEM((nb, nchunks + cap, width), f32),
            pltpu.VMEM((nb, live + tail, width), f32),
            pltpu.SMEM((8 * tops,), jnp.int32),
            pltpu.VMEM((tops, rows, width), f32),
            pltpu.VMEM((tops, 16, width), jnp.int32),
            pltpu.SMEM((tops, 16, width), jnp.int32),
            pltpu.VMEM((nb, nchunks, width), jnp.int32),
            pltpu.SMEM((nb, nchunks, width), jnp.int32),
            pltpu.SemaphoreType.DMA((2,)),
        ],
        compiler_params=pltpu.CompilerParams(vmem_limit_bytes=LIMIT_B),
        name="smooth",
    )(*in_vmem(held, arrived), prior, *in_vmem(*model))


def permuted(x, mask):
    count = lax.axis_size("tm")
    return lax.ppermute(x, "tm", [(i, i ^ mask) for i in range(count)])


def shards(observations, outage_mask, group_length, prior_mean, transition, filter_gain, smoother_gain):
    cap = observations.shape[0]
    nblocks, width = transition.shape[0], transition.shape[1]
    bits = lax.axis_size("tm").bit_length() - 1
    nb = nblocks >> EXCHANGED
    live = (cap << bits) * 3 // 4
    half = nb * cap

    def blocks_of():
        return [held_block(lax.axis_index("tm"), bits, 0, top) for top in range(nb)]

    masks = (3, 5, 6)
    keep, send = pack(bits, observations, outage_mask, group_length, width)
    package = (2 * half + 8, width)
    dealt = local(deal_kernel, [package] * 4, "deal", keep, permuted(send, 1))
    crossed = [permuted(p, mask) for p, mask in zip(dealt[1:], masks)]
    joined = (8 * half + 16, width)
    gain, step, pair, back, row2, col2, power = prepare(
        blocks_of, nb, transition, filter_gain, smoother_gain, dealt[0]
    )
    (held,) = local(join_kernel, [joined], "join", gain, dealt[0], *crossed)
    held = held.reshape(1, *joined)
    arrived = permuted(held, (1 << EXCHANGED) | 1)
    for k in range(EXCHANGED + 1, bits):
        held = jnp.concatenate([held, arrived])
        arrived = permuted(held, (1 << k) | 1)
    rowprod, colprod, powers = products(live, pair, row2, col2, power, held)
    model = [gain, step, pair, rowprod, colprod, back, powers]
    stay, leave = smooth(bits, blocks_of, nb, cap, live, held, arrived, prior_mean.reshape(nblocks, width), model)
    split = local(split_kernel, [(2 * half, width)] * 4, "split", stay, permuted(leave, 1))
    crossed = [permuted(p, mask) for p, mask in zip(split[1:], masks)]
    return place(bits, observations.shape, split[0], *crossed)


def solution(mesh):
    placed = (
        P(("parts", "tm"), None),
        P(("parts", "tm"), None),
        P(("parts", "tm")),
        P("parts"),
        P(),
        P(),
        P(),
    )
    return jax.shard_map(
        shards, mesh=mesh, in_specs=placed, out_specs=P(("parts", "tm"), None), check_vma=False
    )
```

```python
import functools

import jax
import jax.numpy as jnp
from jax import lax
from jax.experimental import pallas as pl
from jax.experimental.pallas import tpu as pltpu
from jax.sharding import PartitionSpec as P

f32 = jnp.float32
bf16 = jnp.bfloat16
LIMIT_P = 2 * 1024 * 1024
LIMIT_A = 8 * 1024 * 1024
LIMIT_B = 8 * 1024 * 1024


def halves(x):
    high = x.astype(bf16)
    return high, (x - high.astype(f32)).astype(bf16)


def left(x):
    high = x.astype(bf16).astype(f32)
    both = jnp.concatenate([high, x - high], axis=0).astype(bf16)
    return jnp.concatenate([both, both], axis=1)


def right(w):
    return jnp.concatenate(halves(w), axis=0)


def dot(a, b):
    both = jnp.dot(a, b, preferred_element_type=f32)
    half = both.shape[0] // 2
    return both[:half] + both[half:]


def mul(x, w):
    return dot(left(x), right(w))


def side(mats):
    return jnp.concatenate(mats, axis=1)


def below(mats):
    return jnp.concatenate(mats, axis=0)


def pick2(wide, seen, width):
    return jnp.where(seen, wide[:, width:], wide[:, :width])


def pick4(wide, first, second, width):
    return jnp.where(
        first,
        pick2(wide[:, 2 * width :], second, width),
        pick2(wide[:, : 2 * width], second, width),
    )


def shift_levels(live):
    levels = []
    unit = 1
    while unit < live:
        levels.append([unit * m for m in (1, 2, 3) if unit * m < live])
        unit *= 4
    return levels


EXCHANGED = 3
PLACED = (0, 2, 3, 1)


def parity(value, bits):
    total = value & 1
    for k in range(1, bits):
        total = total ^ ((value >> k) & 1)
    return total


def held_block(me, bits, rel, top):
    one = ((me >> 1) & 1) ^ ((rel >> 1) & 1)
    two = ((me >> 2) & 1) ^ ((rel >> 2) & 1)
    low = parity(me, bits) ^ (rel & 1) ^ one ^ two ^ parity(top, 8)
    return low + 2 * one + 4 * two + 8 * top


def in_hbm(*arrays):
    return [pltpu.with_memory_space_constraint(a, pltpu.HBM) for a in arrays]


def in_vmem(*arrays):
    return [pltpu.with_memory_space_constraint(a, pltpu.VMEM) for a in arrays]


def local(kernel, shapes, name, *arrays):
    vmem = pl.BlockSpec(memory_space=pltpu.VMEM)
    return pl.pallas_call(
        kernel,
        out_shape=[pltpu.VMEM(shape, f32) for shape in shapes],
        in_specs=[vmem if a.dtype != bf16 else pl.BlockSpec(memory_space=pl.ANY) for a in arrays],
        out_specs=[vmem] * len(shapes),
        compiler_params=pltpu.CompilerParams(vmem_limit_bytes=LIMIT_P),
        name=name,
    )(*in_vmem(*arrays))


def fetch_kernel(x_hbm, mask_hbm, x_ref, mask_ref, sems):
    copies = [
        pltpu.make_async_copy(x_hbm, x_ref, sems.at[0]),
        pltpu.make_async_copy(mask_hbm, mask_ref, sems.at[1]),
    ]
    for c in copies:
        c.start()
    for c in copies:
        c.wait()


def fetch(observations, outage_mask):
    return pl.pallas_call(
        fetch_kernel,
        out_shape=[pltpu.VMEM(observations.shape, f32), pltpu.VMEM(outage_mask.shape, jnp.int32)],
        in_specs=[pl.BlockSpec(memory_space=pltpu.HBM)] * 2,
        out_specs=[pl.BlockSpec(memory_space=pltpu.VMEM)] * 2,
        scratch_shapes=[pltpu.SemaphoreType.DMA((2,))],
        compiler_params=pltpu.CompilerParams(vmem_limit_bytes=LIMIT_P),
        cost_estimate=pl.CostEstimate(flops=0, bytes_accessed=10**6, transcendentals=0),
        name="fetch",
    )(*in_hbm(observations, outage_mask))


def deal_kernel(bits, x_ref, other_ref, length_ref, other_length_ref, mask_ref, other_mask_ref, *outs):
    cap, nblocks = mask_ref.shape
    width = length_ref.shape[1]
    half = (outs[0].shape[0] - 8) // 2
    me = lax.axis_index("tm")
    lane = lax.broadcasted_iota(jnp.int32, (cap, width), 1)
    row = lax.broadcasted_iota(jnp.int32, (cap, width), 0)
    lines = []
    for ref, length in ((mask_ref, length_ref), (other_mask_ref, other_length_ref)):
        wide = jnp.concatenate([ref[...].astype(f32)] * (width // nblocks), axis=1)
        lines.append(jnp.sum(jnp.where(lane // nblocks == row, wide, f32(0.0)), axis=0, keepdims=True))
        lines.append(length[0:1])
    meta = jnp.concatenate(lines + [jnp.zeros((4, width), f32)], axis=0)
    for k, out in enumerate(outs):
        for top in range(half // cap):
            b = held_block(me, bits, 2 * k, top)
            spot = pl.ds(pl.multiple_of(b * width, width), width)
            out[top * cap : (top + 1) * cap] = x_ref[:, spot]
            out[half + top * cap : half + (top + 1) * cap] = other_ref[:, spot]
        out[2 * half :] = meta


def join_kernel(_, *refs):
    out_ref = refs[-1]
    rows = refs[0].shape[0] - 8
    for k, ref in enumerate(refs[:-1]):
        out_ref[k * rows : (k + 1) * rows] = ref[:rows]
        out_ref[3 * rows + 4 * k : 3 * rows + 4 * k + 4] = ref[rows : rows + 4]


def split_kernel(stay_ref, came_ref, *outs):
    half = outs[0].shape[0] // 2
    for k, out in enumerate(outs):
        out[:half] = stay_ref[k * half : (k + 1) * half]
        out[half:] = came_ref[k * half : (k + 1) * half]


def place_kernel(bits, *refs):
    out_ref = refs[-1]
    cap = out_ref.shape[0]
    width = refs[0].shape[1]
    tops = refs[0].shape[0] // (2 * cap)
    me = lax.axis_index("tm")
    for rel in range(1 << EXCHANGED):
        for top in range(tops):
            row = ((rel & 1) * tops + top) * cap
            b = held_block(me, bits, rel, top)
            out_ref[:, pl.ds(pl.multiple_of(b * width, width), width)] = refs[PLACED.index(rel >> 1)][row : row + cap]


def place(bits, shape, *arrays):
    vmem = pl.BlockSpec(memory_space=pltpu.VMEM)
    return pl.pallas_call(
        functools.partial(place_kernel, bits),
        out_shape=jax.ShapeDtypeStruct(shape, f32),
        in_specs=[vmem] * len(arrays),
        out_specs=vmem,
        compiler_params=pltpu.CompilerParams(vmem_limit_bytes=LIMIT_P),
        name="place",
    )(*in_vmem(*arrays))


def model_kernel(
    blocks_of,
    t_hbm,
    k_hbm,
    s_hbm,
    after_ref,
    gain_ref,
    step_ref,
    pair_ref,
    back_ref,
    row_ref,
    col_ref,
    power_ref,
    t_ref,
    k_ref,
    s_ref,
    sems,
):
    nb, width = t_ref.shape[0], t_ref.shape[1]
    copies = []
    for j, b in enumerate(blocks_of()):
        for n, (src, dst) in enumerate(((t_hbm, t_ref), (k_hbm, k_ref), (s_hbm, s_ref))):
            copies.append(pltpu.make_async_copy(src.at[b], dst.at[j], sems.at[j, n]))
    for c in copies:
        c.start()
    for c in copies:
        c.wait()
    eye = (
        lax.broadcasted_iota(jnp.int32, (width, width), 0)
        == lax.broadcasted_iota(jnp.int32, (width, width), 1)
    ).astype(f32)
    both = range(nb)
    rt = [t_ref[j].T for j in both]
    for j in both:
        power_ref[j] = s_ref[j].T
        gain_ref[j] = right(k_ref[j])
    ru = [rt[j] - dot(left(rt[j]), gain_ref[j]) for j in both]
    u = [t_ref[j] - mul(k_ref[j], t_ref[j]) for j in both]
    for j in both:
        step_ref[j] = right(side([rt[j], ru[j]]))
    row2 = [dot(left(below([rt[j], ru[j]])), step_ref[j]) for j in both]
    col2 = [mul(below([t_ref[j], u[j]]), side([t_ref[j], u[j]])) for j in both]
    for j in both:
        back_ref[j] = right(eye - mul(rt[j], power_ref[j]))
        for a in (0, 1):
            for b in (0, 1):
                one, two = slice(a * width, (a + 1) * width), slice(b * width, (b + 1) * width)
                row_ref[j, (2 * a + b) * width : (2 * a + b + 1) * width] = row2[j][one, two]
                col_ref[j, (2 * a + b) * width : (2 * a + b + 1) * width] = col2[j][two, one]
        pair_ref[j] = right(side([row_ref[j, n * width : (n + 1) * width] for n in range(4)]))


def product_kernel(live, pair_ref, row_ref, col_ref, gain_ref, after_ref, rowprod_ref, colprod_ref, power_ref):
    nb, _, width = row_ref.shape
    levels = shift_levels(live)
    both = range(nb)
    power = [gain_ref[j] for j in both]
    for j in both:
        row4 = dot(left(row_ref[j]), pair_ref[j])
        col4 = mul(col_ref[j], side([col_ref[j, n * width : (n + 1) * width] for n in range(4)]))
        for p in range(4):
            for q in range(4):
                rowprod_ref[j, 4 * p + q] = row4[p * width : (p + 1) * width, q * width : (q + 1) * width]
                colprod_ref[j, 4 * p + q] = col4[q * width : (q + 1) * width, p * width : (p + 1) * width]
    for n, level in enumerate(levels):
        rights = [[right(power[j])] for j in both]
        if len(level) > 1:
            second = [dot(left(power[j]), rights[j][0]) for j in both]
            for j in both:
                rights[j].append(right(second[j]))
            double = [dot(left(second[j]), side(rights[j])) for j in both]
            for j in both:
                rights[j].append(right(double[j][:, :width]))
                power[j] = double[j][:, width:]
        for j in both:
            for m in range(len(level)):
                power_ref[j, n, m * 2 * width : (m + 1) * 2 * width] = rights[j][m]


def prepare(blocks_of, nb, transition, filter_gain, smoother_gain, after):
    width = transition.shape[1]
    hbm = pl.BlockSpec(memory_space=pltpu.HBM)
    vmem = pl.BlockSpec(memory_space=pltpu.VMEM)
    return pl.pallas_call(
        functools.partial(model_kernel, blocks_of),
        out_shape=[
            pltpu.VMEM((nb, 2 * width, width), bf16),
            pltpu.VMEM((nb, 2 * width, 2 * width), bf16),
            pltpu.VMEM((nb, 2 * width, 4 * width), bf16),
            pltpu.VMEM((nb, 2 * width, width), bf16),
            pltpu.VMEM((nb, 4 * width, width), f32),
            pltpu.VMEM((nb, 4 * width, width), f32),
            pltpu.VMEM((nb, width, width), f32),
        ],
        in_specs=[hbm] * 3 + [pl.BlockSpec(memory_space=pl.ANY)],
        out_specs=[vmem] * 7,
        scratch_shapes=[
            pltpu.VMEM((nb, width, width), f32),
            pltpu.VMEM((nb, width, width), f32),
            pltpu.VMEM((nb, width, width), f32),
            pltpu.SemaphoreType.DMA((nb, 3)),
        ],
        compiler_params=pltpu.CompilerParams(vmem_limit_bytes=LIMIT_A),
        cost_estimate=pl.CostEstimate(flops=10**9, bytes_accessed=4 * 10**6, transcendentals=0),
        name="prepare",
    )(*in_hbm(transition, filter_gain, smoother_gain), after)


def products(live, pair, row2, col2, gain, after):
    nb, _, width = row2.shape
    levels = shift_levels(live)
    vmem = pl.BlockSpec(memory_space=pltpu.VMEM)
    return pl.pallas_call(
        functools.partial(product_kernel, live),
        out_shape=[
            pltpu.VMEM((nb, 16, width, width), f32),
            pltpu.VMEM((nb, 16, width, width), f32),
            pltpu.VMEM((nb, len(levels), 6 * width, width), bf16),
        ],
        in_specs=[vmem] * 4 + [pl.BlockSpec(memory_space=pl.ANY)],
        out_specs=[vmem] * 3,
        compiler_params=pltpu.CompilerParams(vmem_limit_bytes=LIMIT_A),
        cost_estimate=pl.CostEstimate(flops=10**9, bytes_accessed=4 * 10**6, transcendentals=0),
        name="products",
    )(*in_vmem(pair, row2, col2, gain), after)


def smoother_kernel(
    bits,
    blocks_of,
    live,
    nsent,
    *refs,
):
    smoother_body(bits, blocks_of, live, refs[:nsent], *refs[nsent:])


def smoother_body(
    bits,
    blocks_of,
    live,
    sent_refs,
    prior_ref,
    k_ref,
    step_ref,
    pair_ref,
    rowprod_ref,
    colprod_ref,
    back_ref,
    power_ref,
    stay_ref,
    leave_ref,
    gain_ref,
    seen_ref,
    col_ref,
    colgain_ref,
    start_ref,
    filt_ref,
    starts_smem,
    y_ref,
    meta_ref,
    meta_smem,
    order_ref,
    order_smem,
    sems,
):
    nb, width = gain_ref.shape[0], y_ref.shape[2]
    nblocks = prior_ref.shape[0]
    groups = 8 * y_ref.shape[0]
    cap = stay_ref.shape[0] // (4 * nb)
    meta_row = 8 * nb * cap
    nchunks = live // 4
    levels = shift_levels(live)
    blocks = blocks_of()
    me = lax.axis_index("tm")
    odd = parity(me, bits)

    part = 2 * nb * cap
    for top in range(y_ref.shape[0]):
        most, last = sent_refs[2 * top], sent_refs[2 * top + 1]
        y_ref[top, meta_row : meta_row + 12] = most[3 * part : 3 * part + 12]
        y_ref[top, meta_row + 12 :] = last[part : part + 4]
    meta_ref[...] = y_ref[:, meta_row:].astype(jnp.int32)
    fetch = pltpu.make_async_copy(meta_ref, meta_smem, sems.at[0])
    fetch.start()
    for top in range(y_ref.shape[0]):
        most, last = sent_refs[2 * top], sent_refs[2 * top + 1]
        y_ref[top, : 3 * part] = most[: 3 * part]
        y_ref[top, 3 * part : meta_row] = last[:part]
    places = []
    for g in range(groups):
        d = me ^ g
        places.append((d >> 3, (d >> 1) & 3, odd ^ parity(g, bits)))

    ones = jnp.ones((width, width), bf16)
    lanes = lax.broadcasted_iota(jnp.int32, (cap, width), 1)
    rows = lax.broadcasted_iota(jnp.int32, (cap, width), 0)
    packed = []
    for j, b in enumerate(blocks):
        readings = below(
            [
                y_ref[top, pl.ds(pl.multiple_of(((k * 2 + near) * nb + j) * cap, cap), cap), :]
                for top, k, near in places
            ]
        )
        gains = dot(left(readings), k_ref[j])
        chosen = lanes == rows * nblocks + b
        marks = below(
            [
                jnp.where(
                    chosen,
                    jnp.broadcast_to(y_ref[top, pl.ds(meta_row + 4 * k + 2 * near, 1), :], (cap, width)),
                    f32(0.0),
                )
                for top, k, near in places
            ]
        )
        seen = jnp.dot(marks.astype(bf16), ones, preferred_element_type=f32)
        gains = jnp.where(seen > 0.5, gains, f32(0.0))
        packed.append((gains, seen))
    fetch.wait()
    starts = [0]
    for g in range(groups):
        top, k, near = places[g]
        starts_smem[g] = starts[g]
        starts.append(starts[-1] + meta_smem[top, 4 * k + 2 * near + 1, 0])
    for j, (gains, seen) in enumerate(packed):
        for g in range(groups):
            gain_ref[j, pl.ds(starts[g], cap), :] = gains[g * cap : (g + 1) * cap]
            seen_ref[j, pl.ds(starts[g], cap), :] = seen[g * cap : (g + 1) * cap]

    gain = [[gain_ref[j, pl.ds(s, nchunks, stride=4), :] for s in range(4)] for j in range(nb)]
    marks = [[seen_ref[j, pl.ds(s, nchunks, stride=4), :] for s in range(4)] for j in range(nb)]
    for j in range(nb):
        order = ((marks[j][0] * 2.0 + marks[j][1]) * 2.0 + marks[j][2]) * 2.0 + marks[j][3]
        order_ref[j] = order.astype(jnp.int32)
    fetch = pltpu.make_async_copy(order_ref, order_smem, sems.at[1])
    fetch.start()
    seen = [[m > 0.5 for m in marks[j]] for j in range(nb)]
    begun = [
        dot(left(below([gain[j][0], gain[j][2]])), step_ref[j]) for j in range(nb)
    ]
    twos, lasts, fours = [], [], []
    for j in range(nb):
        twos.append(pick2(begun[j][:nchunks], seen[j][1], width) + gain[j][1])
        lasts.append(pick2(begun[j][nchunks:], seen[j][3], width) + gain[j][3])
    wide = [dot(left(twos[j]), pair_ref[j]) for j in range(nb)]
    for j in range(nb):
        four = pick4(wide[j], seen[j][2], seen[j][3], width) + lasts[j]
        filt_ref[j, :nchunks] = four
        pad = -nchunks % width
        padded = below([four, jnp.zeros((pad, width), f32)]) if pad else four
        for n in range(padded.shape[0] // width):
            colgain_ref[j, n] = padded[n * width : (n + 1) * width].T
        start_ref[j, pl.ds(0, 1), :] = prior_ref[pl.ds(blocks[j], 1), :]
    fetch.wait()

    lane_full = lax.broadcasted_iota(jnp.int32, (width, width), 1)

    def pattern(j, c):
        return order_smem[j, c, 0]

    def two_steps(i, state):
        moved = []
        c = 2 * i
        part = c // width
        lane = c - part * width
        here = lane_full == lane
        for j in range(nb):
            prod = colprod_ref[j, pattern(j, c)] * state[j]
            prod = prod + jnp.where(here, colgain_ref[j, part], f32(0.0))
            column = jnp.broadcast_to(jnp.sum(prod, axis=1, keepdims=True), (width, width))
            pltpu.store(col_ref.at[j, part], column, mask=here)
            row = jnp.sum(rowprod_ref[j, pattern(j, c + 1)] * column, axis=0, keepdims=True)
            row = row + filt_ref[j, pl.ds(c + 1, 1), :]
            start_ref[j, pl.ds(c + 2, 1), :] = row
            moved.append(row)
        return tuple(moved)

    lax.fori_loop(0, nchunks // 2, two_steps, tuple(prior_ref[pl.ds(b, 1), :] for b in blocks))

    for j in range(nb):
        for n in range(col_ref.shape[1]):
            count = min(width, nchunks - n * width) // 2
            flipped = col_ref[j, n].T
            col_ref[j, n] = flipped
            start_ref[j, pl.ds(n * width + 1, count, stride=2), :] = col_ref[j, n, pl.ds(0, count, stride=2), :]
    lefts = [left(start_ref[j, :nchunks]) for j in range(nb)]
    ones = [dot(lefts[j], step_ref[j]) for j in range(nb)]
    pairs = [dot(lefts[j], pair_ref[j]) for j in range(nb)]
    pairs = [pick4(pairs[j], seen[j][0], seen[j][1], width) + twos[j] for j in range(nb)]
    threes = [dot(left(pairs[j]), step_ref[j]) for j in range(nb)]
    for j in range(nb):
        one = pick2(ones[j], seen[j][0], width) + gain[j][0]
        three = pick2(threes[j], seen[j][2], width) + gain[j][2]
        four = start_ref[j, 1 : nchunks + 1]
        for s, value in enumerate((one, pairs[j], three, four)):
            filt_ref[j, pl.ds(s, nchunks, stride=4), :] = value
    is_last = lax.broadcasted_iota(jnp.int32, (live, width), 0) == live - 1
    tail = filt_ref.shape[1] - live
    filtered = [filt_ref[j, :live] for j in range(nb)]
    smoothed = [jnp.where(is_last, x, dot(left(x), back_ref[j])) for j, x in enumerate(filtered)]
    for j in range(nb):
        filt_ref[j, live:] = jnp.zeros((tail, width), f32)
    for n, level in enumerate(levels):
        for j in range(nb):
            filt_ref[j, :live] = smoothed[j]
        for j in range(nb):
            moved = side([left(filt_ref[j, sh : sh + live]) for sh in level])
            smoothed[j] = smoothed[j] + dot(moved, power_ref[j, n, : 2 * width * len(level)])
    for j in range(nb):
        filt_ref[j, :live] = smoothed[j]
    for j in range(nb):
        for d in range(1 << EXCHANGED):
            near = parity(d, EXCHANGED)
            value = filt_ref[j, pl.ds(starts_smem[me ^ d], cap), :]
            value = jnp.where(rows < meta_smem[0, 4 * (d >> 1) + 2 * near + 1, 0], value, f32(0.0))
            row = ((d >> 1) * nb + j) * cap
            (leave_ref if near else stay_ref)[row : row + cap] = value


def smooth(bits, blocks_of, nb, cap, live, sent, prior, model):
    tops = len(sent) // 2
    width = sent[0].shape[1]
    rows = 8 * nb * cap + 16
    nchunks = live // 4
    levels = shift_levels(live)
    parts = -(-nchunks // width)
    vmem = pl.BlockSpec(memory_space=pltpu.VMEM)
    tail = max(max(level) for level in levels) + cap
    return pl.pallas_call(
        functools.partial(smoother_kernel, bits, blocks_of, live, len(sent)),
        out_shape=[pltpu.VMEM((4 * nb * cap, width), f32)] * 2,
        in_specs=[vmem] * (len(sent) + 8),
        out_specs=[vmem] * 2,
        scratch_shapes=[
            pltpu.VMEM((nb, live + cap, width), f32),
            pltpu.VMEM((nb, live + cap, width), f32),
            pltpu.VMEM((nb, parts, width, width), f32),
            pltpu.VMEM((nb, parts, width, width), f32),
            pltpu.VMEM((nb, nchunks + cap, width), f32),
            pltpu.VMEM((nb, live + tail, width), f32),
            pltpu.SMEM((8 * tops,), jnp.int32),
            pltpu.VMEM((tops, rows, width), f32),
            pltpu.VMEM((tops, 16, width), jnp.int32),
            pltpu.SMEM((tops, 16, width), jnp.int32),
            pltpu.VMEM((nb, nchunks, width), jnp.int32),
            pltpu.SMEM((nb, nchunks, width), jnp.int32),
            pltpu.SemaphoreType.DMA((2,)),
        ],
        compiler_params=pltpu.CompilerParams(vmem_limit_bytes=LIMIT_B),
        name="smooth",
    )(*in_vmem(*sent), prior, *in_vmem(*model))


def permuted(x, mask):
    count = lax.axis_size("tm")
    return lax.ppermute(x, "tm", [(i, i ^ mask) for i in range(count)])


def shards(observations, outage_mask, group_length, prior_mean, transition, filter_gain, smoother_gain):
    cap = observations.shape[0]
    nblocks, width = transition.shape[0], transition.shape[1]
    bits = lax.axis_size("tm").bit_length() - 1
    nb = nblocks >> EXCHANGED
    live = (cap << bits) * 3 // 4
    half = nb * cap

    def blocks_of():
        return [held_block(lax.axis_index("tm"), bits, 0, top) for top in range(nb)]

    masks = (3, 5, 6)
    package = (2 * half + 8, width)
    other = permuted(observations, 1), permuted(outage_mask, 1)
    length = jnp.broadcast_to(group_length.astype(f32)[:, None], (8, width))
    own = fetch(observations, outage_mask)
    dealt = local(
        functools.partial(deal_kernel, bits),
        [package] * 4,
        "deal",
        own[0],
        other[0],
        length,
        permuted(length, 1),
        own[1],
        other[1],
    )
    crossed = [permuted(p, mask) for p, mask in zip(dealt[1:], masks)]
    gain, step, pair, back, row2, col2, power = prepare(
        blocks_of, nb, transition, filter_gain, smoother_gain, dealt[0]
    )
    sent = [*local(join_kernel, [(6 * half + 16, width)], "join", gain, dealt[0], *crossed[:2]), crossed[2]]
    for k in range(EXCHANGED, bits):
        sent = sent + [permuted(x, (1 << k) | 1) for x in sent]
    rowprod, colprod, powers = products(live, pair, row2, col2, power, crossed[2])
    model = [gain, step, pair, rowprod, colprod, back, powers]
    stay, leave = smooth(bits, blocks_of, nb, cap, live, sent, prior_mean.reshape(nblocks, width), model)
    split = local(split_kernel, [(2 * half, width)] * 4, "split", stay, permuted(leave, 1))
    crossed = [split[0]] + [permuted(p, mask) for p, mask in zip(split[1:], masks)]
    return place(bits, observations.shape, *(crossed[k] for k in PLACED))


def solution(mesh):
    placed = (
        P(("parts", "tm"), None),
        P(("parts", "tm"), None),
        P(("parts", "tm")),
        P("parts"),
        P(),
        P(),
        P(),
    )
    return jax.shard_map(
        shards, mesh=mesh, in_specs=placed, out_specs=P(("parts", "tm"), None), check_vma=False
    )
```

```python
import functools

import jax
import jax.numpy as jnp
from jax import lax
from jax.experimental import pallas as pl
from jax.experimental.pallas import tpu as pltpu
from jax.sharding import PartitionSpec as P

f32 = jnp.float32
bf16 = jnp.bfloat16
LIMIT_P = 2 * 1024 * 1024
LIMIT_A = 8 * 1024 * 1024
LIMIT_B = 8 * 1024 * 1024


def halves(x):
    high = x.astype(bf16)
    return high, (x - high.astype(f32)).astype(bf16)


def left(x):
    high = x.astype(bf16).astype(f32)
    both = jnp.concatenate([high, x - high], axis=0).astype(bf16)
    return jnp.concatenate([both, both], axis=1)


def right(w):
    return jnp.concatenate(halves(w), axis=0)


def dot(a, b):
    both = jnp.dot(a, b, preferred_element_type=f32)
    half = both.shape[0] // 2
    return both[:half] + both[half:]


def mul(x, w):
    return dot(left(x), right(w))


def side(mats):
    return jnp.concatenate(mats, axis=1)


def below(mats):
    return jnp.concatenate(mats, axis=0)


def pick2(wide, seen, width):
    return jnp.where(seen, wide[:, width:], wide[:, :width])


def pick4(wide, first, second, width):
    return jnp.where(
        first,
        pick2(wide[:, 2 * width :], second, width),
        pick2(wide[:, : 2 * width], second, width),
    )


def shift_levels(live):
    levels = []
    unit = 1
    while unit < live:
        levels.append([unit * m for m in (1, 2, 3) if unit * m < live])
        unit *= 4
    return levels


EXCHANGED = 3
PARTS = ((0,), (1, 2, 3))
PLACED = (0, 2, 3, 1)


def parity(value, bits):
    total = value & 1
    for k in range(1, bits):
        total = total ^ ((value >> k) & 1)
    return total


def held_block(me, bits, rel, top):
    one = ((me >> 1) & 1) ^ ((rel >> 1) & 1)
    two = ((me >> 2) & 1) ^ ((rel >> 2) & 1)
    low = parity(me, bits) ^ (rel & 1) ^ one ^ two ^ parity(top, 8)
    return low + 2 * one + 4 * two + 8 * top


def in_hbm(*arrays):
    return [pltpu.with_memory_space_constraint(a, pltpu.HBM) for a in arrays]


def in_vmem(*arrays):
    return [pltpu.with_memory_space_constraint(a, pltpu.VMEM) for a in arrays]


def local(kernel, shapes, name, *arrays):
    vmem = pl.BlockSpec(memory_space=pltpu.VMEM)
    return pl.pallas_call(
        kernel,
        out_shape=[pltpu.VMEM(shape, f32) for shape in shapes],
        in_specs=[vmem if a.dtype != bf16 else pl.BlockSpec(memory_space=pl.ANY) for a in arrays],
        out_specs=[vmem] * len(shapes),
        compiler_params=pltpu.CompilerParams(vmem_limit_bytes=LIMIT_P),
        name=name,
    )(*in_vmem(*arrays))


def fetch_kernel(blocks_of, x_hbm, mask_hbm, t_hbm, k_hbm, s_hbm, x_ref, mask_ref, t_ref, k_ref, s_ref, sems):
    copies = [
        pltpu.make_async_copy(x_hbm, x_ref, sems.at[0]),
        pltpu.make_async_copy(mask_hbm, mask_ref, sems.at[1]),
    ]
    for j, b in enumerate(blocks_of()):
        for n, (src, dst) in enumerate(((t_hbm, t_ref), (k_hbm, k_ref), (s_hbm, s_ref))):
            copies.append(pltpu.make_async_copy(src.at[b], dst.at[j], sems.at[2 + 3 * j + n]))
    for c in copies:
        c.start()
    for c in copies:
        c.wait()


def fetch(blocks_of, nb, observations, outage_mask, *mats):
    width = mats[0].shape[1]
    return pl.pallas_call(
        functools.partial(fetch_kernel, blocks_of),
        out_shape=[
            pltpu.VMEM(observations.shape, f32),
            pltpu.VMEM(outage_mask.shape, jnp.int32),
        ]
        + [pltpu.VMEM((nb, width, width), f32)] * 3,
        in_specs=[pl.BlockSpec(memory_space=pltpu.HBM)] * 5,
        out_specs=[pl.BlockSpec(memory_space=pltpu.VMEM)] * 5,
        scratch_shapes=[pltpu.SemaphoreType.DMA((2 + 3 * nb,))],
        compiler_params=pltpu.CompilerParams(vmem_limit_bytes=LIMIT_P),
        cost_estimate=pl.CostEstimate(flops=0, bytes_accessed=10**6, transcendentals=0),
        name="fetch",
    )(*in_hbm(observations, outage_mask, *mats))


def deal_kernel(bits, x_ref, other_ref, mask_ref, other_mask_ref, length_ref, other_length_ref, *outs):
    cap, nblocks = mask_ref.shape
    width = length_ref.shape[1]
    half = (outs[0].shape[0] - 8) // 2
    me = lax.axis_index("tm")
    lane = lax.broadcasted_iota(jnp.int32, (cap, width), 1)
    row = lax.broadcasted_iota(jnp.int32, (cap, width), 0)
    lines = []
    for ref, length in ((mask_ref, length_ref), (other_mask_ref, other_length_ref)):
        wide = jnp.concatenate([ref[...].astype(f32)] * (width // nblocks), axis=1)
        lines.append(jnp.sum(jnp.where(lane // nblocks == row, wide, f32(0.0)), axis=0, keepdims=True))
        lines.append(length[0:1])
    meta = jnp.concatenate(lines + [jnp.zeros((4, width), f32)], axis=0)
    for k, out in enumerate(outs):
        for top in range(half // cap):
            b = held_block(me, bits, 2 * k, top)
            spot = pl.ds(pl.multiple_of(b * width, width), width)
            out[top * cap : (top + 1) * cap] = x_ref[:, spot]
            out[half + top * cap : half + (top + 1) * cap] = other_ref[:, spot]
        out[2 * half :] = meta


def join_kernel(_, *refs):
    out_ref = refs[-1]
    rows = refs[0].shape[0] - 8
    count = len(refs) - 1
    for k, ref in enumerate(refs[:-1]):
        out_ref[k * rows : (k + 1) * rows] = ref[:rows]
        out_ref[count * rows + 4 * k : count * rows + 4 * k + 4] = ref[rows : rows + 4]


def split_kernel(stay_ref, came_ref, *outs):
    half = outs[0].shape[0] // 2
    for k, out in enumerate(outs):
        out[:half] = stay_ref[k * half : (k + 1) * half]
        out[half:] = came_ref[k * half : (k + 1) * half]


def place_kernel(bits, *refs):
    out_ref = refs[-1]
    cap = out_ref.shape[0]
    width = refs[0].shape[1]
    tops = refs[0].shape[0] // (2 * cap)
    me = lax.axis_index("tm")
    for rel in range(1 << EXCHANGED):
        for top in range(tops):
            row = ((rel & 1) * tops + top) * cap
            b = held_block(me, bits, rel, top)
            out_ref[:, pl.ds(pl.multiple_of(b * width, width), width)] = refs[PLACED.index(rel >> 1)][row : row + cap]


def place(bits, shape, *arrays):
    vmem = pl.BlockSpec(memory_space=pltpu.VMEM)
    return pl.pallas_call(
        functools.partial(place_kernel, bits),
        out_shape=jax.ShapeDtypeStruct(shape, f32),
        in_specs=[vmem] * len(arrays),
        out_specs=vmem,
        compiler_params=pltpu.CompilerParams(vmem_limit_bytes=LIMIT_P),
        name="place",
    )(*in_vmem(*arrays))


def model_kernel(
    t_ref,
    k_ref,
    s_ref,
    after_ref,
    gain_ref,
    step_ref,
    pair_ref,
    back_ref,
    row_ref,
    col_ref,
    power_ref,
):
    nb, width = t_ref.shape[0], t_ref.shape[1]
    eye = (
        lax.broadcasted_iota(jnp.int32, (width, width), 0)
        == lax.broadcasted_iota(jnp.int32, (width, width), 1)
    ).astype(f32)
    both = range(nb)
    rt = [t_ref[j].T for j in both]
    for j in both:
        power_ref[j] = s_ref[j].T
        gain_ref[j] = right(k_ref[j])
    ru = [rt[j] - dot(left(rt[j]), gain_ref[j]) for j in both]
    u = [t_ref[j] - mul(k_ref[j], t_ref[j]) for j in both]
    for j in both:
        step_ref[j] = right(side([rt[j], ru[j]]))
    row2 = [dot(left(below([rt[j], ru[j]])), step_ref[j]) for j in both]
    col2 = [mul(below([t_ref[j], u[j]]), side([t_ref[j], u[j]])) for j in both]
    for j in both:
        back_ref[j] = right(eye - mul(rt[j], power_ref[j]))
        for a in (0, 1):
            for b in (0, 1):
                one, two = slice(a * width, (a + 1) * width), slice(b * width, (b + 1) * width)
                row_ref[j, (2 * a + b) * width : (2 * a + b + 1) * width] = row2[j][one, two]
                col_ref[j, (2 * a + b) * width : (2 * a + b + 1) * width] = col2[j][two, one]
        pair_ref[j] = right(side([row_ref[j, n * width : (n + 1) * width] for n in range(4)]))


def product_kernel(live, pair_ref, row_ref, col_ref, gain_ref, after_ref, rowprod_ref, colprod_ref, power_ref):
    nb, _, width = row_ref.shape
    levels = shift_levels(live)
    both = range(nb)
    power = [gain_ref[j] for j in both]
    for j in both:
        row4 = dot(left(row_ref[j]), pair_ref[j])
        col4 = mul(col_ref[j], side([col_ref[j, n * width : (n + 1) * width] for n in range(4)]))
        for p in range(4):
            for q in range(4):
                rowprod_ref[j, 4 * p + q] = row4[p * width : (p + 1) * width, q * width : (q + 1) * width]
                colprod_ref[j, 4 * p + q] = col4[q * width : (q + 1) * width, p * width : (p + 1) * width]
    for n, level in enumerate(levels):
        rights = [[right(power[j])] for j in both]
        if len(level) > 1:
            second = [dot(left(power[j]), rights[j][0]) for j in both]
            for j in both:
                rights[j].append(right(second[j]))
            double = [dot(left(second[j]), side(rights[j])) for j in both]
            for j in both:
                rights[j].append(right(double[j][:, :width]))
                power[j] = double[j][:, width:]
        for j in both:
            for m in range(len(level)):
                power_ref[j, n, m * 2 * width : (m + 1) * 2 * width] = rights[j][m]


def prepare(mats, after):
    nb, width = mats[0].shape[:2]
    vmem = pl.BlockSpec(memory_space=pltpu.VMEM)
    return pl.pallas_call(
        model_kernel,
        out_shape=[
            pltpu.VMEM((nb, 2 * width, width), bf16),
            pltpu.VMEM((nb, 2 * width, 2 * width), bf16),
            pltpu.VMEM((nb, 2 * width, 4 * width), bf16),
            pltpu.VMEM((nb, 2 * width, width), bf16),
            pltpu.VMEM((nb, 4 * width, width), f32),
            pltpu.VMEM((nb, 4 * width, width), f32),
            pltpu.VMEM((nb, width, width), f32),
        ],
        in_specs=[vmem] * 3 + [pl.BlockSpec(memory_space=pl.ANY)],
        out_specs=[vmem] * 7,
        compiler_params=pltpu.CompilerParams(vmem_limit_bytes=LIMIT_A),
        cost_estimate=pl.CostEstimate(flops=10**9, bytes_accessed=4 * 10**6, transcendentals=0),
        name="prepare",
    )(*in_vmem(*mats), after)


def products(live, pair, row2, col2, gain, after):
    nb, _, width = row2.shape
    levels = shift_levels(live)
    vmem = pl.BlockSpec(memory_space=pltpu.VMEM)
    return pl.pallas_call(
        functools.partial(product_kernel, live),
        out_shape=[
            pltpu.VMEM((nb, 16, width, width), f32),
            pltpu.VMEM((nb, 16, width, width), f32),
            pltpu.VMEM((nb, len(levels), 6 * width, width), bf16),
        ],
        in_specs=[vmem] * 4 + [pl.BlockSpec(memory_space=pl.ANY)],
        out_specs=[vmem] * 3,
        compiler_params=pltpu.CompilerParams(vmem_limit_bytes=LIMIT_A),
        cost_estimate=pl.CostEstimate(flops=10**9, bytes_accessed=4 * 10**6, transcendentals=0),
        name="products",
    )(*in_vmem(pair, row2, col2, gain), after)


def smoother_kernel(
    bits,
    blocks_of,
    live,
    nsent,
    *refs,
):
    smoother_body(bits, blocks_of, live, refs[:nsent], *refs[nsent:])


def smoother_body(
    bits,
    blocks_of,
    live,
    sent_refs,
    prior_ref,
    k_ref,
    step_ref,
    pair_ref,
    rowprod_ref,
    colprod_ref,
    back_ref,
    power_ref,
    stay_ref,
    leave_ref,
    gain_ref,
    seen_ref,
    col_ref,
    colgain_ref,
    start_ref,
    filt_ref,
    starts_smem,
    y_ref,
    meta_ref,
    meta_smem,
    order_ref,
    order_smem,
    sems,
):
    nb, width = gain_ref.shape[0], y_ref.shape[2]
    nblocks = prior_ref.shape[0]
    groups = 8 * y_ref.shape[0]
    cap = stay_ref.shape[0] // (4 * nb)
    meta_row = 8 * nb * cap
    nchunks = live // 4
    levels = shift_levels(live)
    blocks = blocks_of()
    me = lax.axis_index("tm")
    odd = parity(me, bits)

    part = 2 * nb * cap
    for n, ref in enumerate(sent_refs):
        spots = PARTS[n % len(PARTS)]
        for i, k in enumerate(spots):
            row = len(spots) * part + 4 * i
            y_ref[n // len(PARTS), meta_row + 4 * k : meta_row + 4 * k + 4] = ref[row : row + 4]
    meta_ref[...] = y_ref[:, meta_row:].astype(jnp.int32)
    fetch = pltpu.make_async_copy(meta_ref, meta_smem, sems.at[0])
    fetch.start()
    for n, ref in enumerate(sent_refs):
        for i, k in enumerate(PARTS[n % len(PARTS)]):
            y_ref[n // len(PARTS), k * part : (k + 1) * part] = ref[i * part : (i + 1) * part]
    places = []
    for g in range(groups):
        d = me ^ g
        places.append((d >> 3, (d >> 1) & 3, odd ^ parity(g, bits)))

    ones = jnp.ones((width, width), bf16)
    lanes = lax.broadcasted_iota(jnp.int32, (cap, width), 1)
    rows = lax.broadcasted_iota(jnp.int32, (cap, width), 0)
    packed = []
    for j, b in enumerate(blocks):
        readings = below(
            [
                y_ref[top, pl.ds(pl.multiple_of(((k * 2 + near) * nb + j) * cap, cap), cap), :]
                for top, k, near in places
            ]
        )
        gains = dot(left(readings), k_ref[j])
        chosen = lanes == rows * nblocks + b
        marks = below(
            [
                jnp.where(
                    chosen,
                    jnp.broadcast_to(y_ref[top, pl.ds(meta_row + 4 * k + 2 * near, 1), :], (cap, width)),
                    f32(0.0),
                )
                for top, k, near in places
            ]
        )
        seen = jnp.dot(marks.astype(bf16), ones, preferred_element_type=f32)
        gains = jnp.where(seen > 0.5, gains, f32(0.0))
        packed.append((gains, seen))
    fetch.wait()
    starts = [0]
    for g in range(groups):
        top, k, near = places[g]
        starts_smem[g] = starts[g]
        starts.append(starts[-1] + meta_smem[top, 4 * k + 2 * near + 1, 0])
    for j, (gains, seen) in enumerate(packed):
        for g in range(groups):
            gain_ref[j, pl.ds(starts[g], cap), :] = gains[g * cap : (g + 1) * cap]
            seen_ref[j, pl.ds(starts[g], cap), :] = seen[g * cap : (g + 1) * cap]

    gain = [[gain_ref[j, pl.ds(s, nchunks, stride=4), :] for s in range(4)] for j in range(nb)]
    marks = [[seen_ref[j, pl.ds(s, nchunks, stride=4), :] for s in range(4)] for j in range(nb)]
    for j in range(nb):
        order = ((marks[j][0] * 2.0 + marks[j][1]) * 2.0 + marks[j][2]) * 2.0 + marks[j][3]
        order_ref[j] = order.astype(jnp.int32)
    fetch = pltpu.make_async_copy(order_ref, order_smem, sems.at[1])
    fetch.start()
    seen = [[m > 0.5 for m in marks[j]] for j in range(nb)]
    begun = [
        dot(left(below([gain[j][0], gain[j][2]])), step_ref[j]) for j in range(nb)
    ]
    twos, lasts, fours = [], [], []
    for j in range(nb):
        twos.append(pick2(begun[j][:nchunks], seen[j][1], width) + gain[j][1])
        lasts.append(pick2(begun[j][nchunks:], seen[j][3], width) + gain[j][3])
    wide = [dot(left(twos[j]), pair_ref[j]) for j in range(nb)]
    for j in range(nb):
        four = pick4(wide[j], seen[j][2], seen[j][3], width) + lasts[j]
        filt_ref[j, :nchunks] = four
        pad = -nchunks % width
        padded = below([four, jnp.zeros((pad, width), f32)]) if pad else four
        for n in range(padded.shape[0] // width):
            colgain_ref[j, n] = padded[n * width : (n + 1) * width].T
        start_ref[j, pl.ds(0, 1), :] = prior_ref[pl.ds(blocks[j], 1), :]
    fetch.wait()

    lane_full = lax.broadcasted_iota(jnp.int32, (width, width), 1)

    def pattern(j, c):
        return order_smem[j, c, 0]

    def two_steps(i, state):
        moved = []
        c = 2 * i
        part = c // width
        lane = c - part * width
        here = lane_full == lane
        for j in range(nb):
            prod = colprod_ref[j, pattern(j, c)] * state[j]
            prod = prod + jnp.where(here, colgain_ref[j, part], f32(0.0))
            column = jnp.broadcast_to(jnp.sum(prod, axis=1, keepdims=True), (width, width))
            pltpu.store(col_ref.at[j, part], column, mask=here)
            row = jnp.sum(rowprod_ref[j, pattern(j, c + 1)] * column, axis=0, keepdims=True)
            row = row + filt_ref[j, pl.ds(c + 1, 1), :]
            start_ref[j, pl.ds(c + 2, 1), :] = row
            moved.append(row)
        return tuple(moved)

    lax.fori_loop(0, nchunks // 2, two_steps, tuple(prior_ref[pl.ds(b, 1), :] for b in blocks))

    for j in range(nb):
        for n in range(col_ref.shape[1]):
            count = min(width, nchunks - n * width) // 2
            flipped = col_ref[j, n].T
            col_ref[j, n] = flipped
            start_ref[j, pl.ds(n * width + 1, count, stride=2), :] = col_ref[j, n, pl.ds(0, count, stride=2), :]
    lefts = [left(start_ref[j, :nchunks]) for j in range(nb)]
    ones = [dot(lefts[j], step_ref[j]) for j in range(nb)]
    pairs = [dot(lefts[j], pair_ref[j]) for j in range(nb)]
    pairs = [pick4(pairs[j], seen[j][0], seen[j][1], width) + twos[j] for j in range(nb)]
    threes = [dot(left(pairs[j]), step_ref[j]) for j in range(nb)]
    for j in range(nb):
        one = pick2(ones[j], seen[j][0], width) + gain[j][0]
        three = pick2(threes[j], seen[j][2], width) + gain[j][2]
        four = start_ref[j, 1 : nchunks + 1]
        for s, value in enumerate((one, pairs[j], three, four)):
            filt_ref[j, pl.ds(s, nchunks, stride=4), :] = value
    is_last = lax.broadcasted_iota(jnp.int32, (live, width), 0) == live - 1
    tail = filt_ref.shape[1] - live
    filtered = [filt_ref[j, :live] for j in range(nb)]
    smoothed = [jnp.where(is_last, x, dot(left(x), back_ref[j])) for j, x in enumerate(filtered)]
    for j in range(nb):
        filt_ref[j, live:] = jnp.zeros((tail, width), f32)
    for n, level in enumerate(levels):
        for j in range(nb):
            filt_ref[j, :live] = smoothed[j]
        for j in range(nb):
            moved = side([left(filt_ref[j, sh : sh + live]) for sh in level])
            smoothed[j] = smoothed[j] + dot(moved, power_ref[j, n, : 2 * width * len(level)])
    for j in range(nb):
        filt_ref[j, :live] = smoothed[j]
    for j in range(nb):
        for d in range(1 << EXCHANGED):
            near = parity(d, EXCHANGED)
            value = filt_ref[j, pl.ds(starts_smem[me ^ d], cap), :]
            value = jnp.where(rows < meta_smem[0, 4 * (d >> 1) + 2 * near + 1, 0], value, f32(0.0))
            row = ((d >> 1) * nb + j) * cap
            (leave_ref if near else stay_ref)[row : row + cap] = value


def smooth(bits, blocks_of, nb, cap, live, sent, prior, model):
    tops = len(sent) // len(PARTS)
    width = sent[0].shape[1]
    rows = 8 * nb * cap + 16
    nchunks = live // 4
    levels = shift_levels(live)
    parts = -(-nchunks // width)
    vmem = pl.BlockSpec(memory_space=pltpu.VMEM)
    tail = max(max(level) for level in levels) + cap
    return pl.pallas_call(
        functools.partial(smoother_kernel, bits, blocks_of, live, len(sent)),
        out_shape=[pltpu.VMEM((4 * nb * cap, width), f32)] * 2,
        in_specs=[vmem] * (len(sent) + 8),
        out_specs=[vmem] * 2,
        scratch_shapes=[
            pltpu.VMEM((nb, live + cap, width), f32),
            pltpu.VMEM((nb, live + cap, width), f32),
            pltpu.VMEM((nb, parts, width, width), f32),
            pltpu.VMEM((nb, parts, width, width), f32),
            pltpu.VMEM((nb, nchunks + cap, width), f32),
            pltpu.VMEM((nb, live + tail, width), f32),
            pltpu.SMEM((8 * tops,), jnp.int32),
            pltpu.VMEM((tops, rows, width), f32),
            pltpu.VMEM((tops, 16, width), jnp.int32),
            pltpu.SMEM((tops, 16, width), jnp.int32),
            pltpu.VMEM((nb, nchunks, width), jnp.int32),
            pltpu.SMEM((nb, nchunks, width), jnp.int32),
            pltpu.SemaphoreType.DMA((2,)),
        ],
        compiler_params=pltpu.CompilerParams(vmem_limit_bytes=LIMIT_B),
        name="smooth",
    )(*in_vmem(*sent), prior, *in_vmem(*model))


def permuted(x, mask):
    count = lax.axis_size("tm")
    return lax.ppermute(x, "tm", [(i, i ^ mask) for i in range(count)])


def shards(observations, outage_mask, group_length, prior_mean, transition, filter_gain, smoother_gain):
    cap = observations.shape[0]
    nblocks, width = transition.shape[0], transition.shape[1]
    bits = lax.axis_size("tm").bit_length() - 1
    nb = nblocks >> EXCHANGED
    live = (cap << bits) * 3 // 4
    half = nb * cap

    def blocks_of():
        return [held_block(lax.axis_index("tm"), bits, 0, top) for top in range(nb)]

    masks = (3, 5, 6)
    package = (2 * half + 8, width)
    other = permuted(observations, 1), permuted(outage_mask, 1)
    length = jnp.broadcast_to(group_length.astype(f32)[:, None], (8, width))
    own = fetch(blocks_of, nb, observations, outage_mask, transition, filter_gain, smoother_gain)
    dealt = local(
        functools.partial(deal_kernel, bits),
        [package] * 4,
        "deal",
        own[0],
        other[0],
        own[1],
        other[1],
        length,
        permuted(length, 1),
    )
    crossed = [permuted(p, mask) for p, mask in zip(dealt[1:], masks)]
    gain, step, pair, back, row2, col2, power = prepare(own[2:], dealt[0])
    held = [dealt[0], *crossed]
    sent = []
    for spots in PARTS:
        if len(spots) == 1:
            sent.append(held[spots[0]])
        else:
            rows = 2 * half * len(spots) + -(-4 * len(spots) // 8) * 8
            sent += local(join_kernel, [(rows, width)], "join", gain, *(held[k] for k in spots))
    for k in range(EXCHANGED, bits):
        sent = sent + [permuted(x, (1 << k) | 1) for x in sent]
    rowprod, colprod, powers = products(live, pair, row2, col2, power, crossed[2])
    model = [gain, step, pair, rowprod, colprod, back, powers]
    stay, leave = smooth(bits, blocks_of, nb, cap, live, sent, prior_mean.reshape(nblocks, width), model)
    split = local(split_kernel, [(2 * half, width)] * 4, "split", stay, permuted(leave, 1))
    crossed = [split[0]] + [permuted(p, mask) for p, mask in zip(split[1:], masks)]
    return place(bits, observations.shape, *(crossed[k] for k in PLACED))


def solution(mesh):
    placed = (
        P(("parts", "tm"), None),
        P(("parts", "tm"), None),
        P(("parts", "tm")),
        P("parts"),
        P(),
        P(),
        P(),
    )
    return jax.shard_map(
        shards, mesh=mesh, in_specs=placed, out_specs=P(("parts", "tm"), None), check_vma=False
    )
```

```python
import functools

import jax
import jax.numpy as jnp
from jax import lax
from jax.experimental import pallas as pl
from jax.experimental.pallas import tpu as pltpu
from jax.sharding import PartitionSpec as P

f32 = jnp.float32
bf16 = jnp.bfloat16
LIMIT_P = 2 * 1024 * 1024
LIMIT_A = 8 * 1024 * 1024
LIMIT_B = 8 * 1024 * 1024


def halves(x):
    high = x.astype(bf16)
    return high, (x - high.astype(f32)).astype(bf16)


def left(x):
    high = x.astype(bf16).astype(f32)
    both = jnp.concatenate([high, x - high], axis=0).astype(bf16)
    return jnp.concatenate([both, both], axis=1)


def right(w):
    return jnp.concatenate(halves(w), axis=0)


def dot(a, b):
    both = jnp.dot(a, b, preferred_element_type=f32)
    half = both.shape[0] // 2
    return both[:half] + both[half:]


def mul(x, w):
    return dot(left(x), right(w))


def side(mats):
    return jnp.concatenate(mats, axis=1)


def below(mats):
    return jnp.concatenate(mats, axis=0)


def pick2(wide, seen, width):
    return jnp.where(seen, wide[:, width:], wide[:, :width])


def pick4(wide, first, second, width):
    return jnp.where(
        first,
        pick2(wide[:, 2 * width :], second, width),
        pick2(wide[:, : 2 * width], second, width),
    )


def shift_levels(live):
    levels = []
    unit = 1
    while unit < live:
        levels.append([unit * m for m in (1, 2, 3) if unit * m < live])
        unit *= 4
    return levels


EXCHANGED = 3
PARTS = ((0,), (3, 1, 2))
PLACED = (0, 2, 3, 1)


def parity(value, bits):
    total = value & 1
    for k in range(1, bits):
        total = total ^ ((value >> k) & 1)
    return total


def held_block(me, bits, rel, top):
    one = ((me >> 1) & 1) ^ ((rel >> 1) & 1)
    two = ((me >> 2) & 1) ^ ((rel >> 2) & 1)
    low = parity(me, bits) ^ (rel & 1) ^ one ^ two ^ parity(top, 8)
    return low + 2 * one + 4 * two + 8 * top


def in_hbm(*arrays):
    return [pltpu.with_memory_space_constraint(a, pltpu.HBM) for a in arrays]


def in_vmem(*arrays):
    return [pltpu.with_memory_space_constraint(a, pltpu.VMEM) for a in arrays]


def local(kernel, shapes, name, *arrays):
    vmem = pl.BlockSpec(memory_space=pltpu.VMEM)
    return pl.pallas_call(
        kernel,
        out_shape=[pltpu.VMEM(shape, f32) for shape in shapes],
        in_specs=[vmem if a.dtype != bf16 else pl.BlockSpec(memory_space=pl.ANY) for a in arrays],
        out_specs=[vmem] * len(shapes),
        compiler_params=pltpu.CompilerParams(vmem_limit_bytes=LIMIT_P),
        name=name,
    )(*in_vmem(*arrays))


def fetch_kernel(blocks_of, x_hbm, mask_hbm, t_hbm, k_hbm, s_hbm, x_ref, mask_ref, t_ref, k_ref, s_ref, sems):
    copies = [
        pltpu.make_async_copy(x_hbm, x_ref, sems.at[0]),
        pltpu.make_async_copy(mask_hbm, mask_ref, sems.at[1]),
    ]
    for j, b in enumerate(blocks_of()):
        for n, (src, dst) in enumerate(((t_hbm, t_ref), (k_hbm, k_ref), (s_hbm, s_ref))):
            copies.append(pltpu.make_async_copy(src.at[b], dst.at[j], sems.at[2 + 3 * j + n]))
    for c in copies:
        c.start()
    for c in copies:
        c.wait()


def fetch(blocks_of, nb, observations, outage_mask, *mats):
    width = mats[0].shape[1]
    return pl.pallas_call(
        functools.partial(fetch_kernel, blocks_of),
        out_shape=[
            pltpu.VMEM(observations.shape, f32),
            pltpu.VMEM(outage_mask.shape, jnp.int32),
        ]
        + [pltpu.VMEM((nb, width, width), f32)] * 3,
        in_specs=[pl.BlockSpec(memory_space=pltpu.HBM)] * 5,
        out_specs=[pl.BlockSpec(memory_space=pltpu.VMEM)] * 5,
        scratch_shapes=[pltpu.SemaphoreType.DMA((2 + 3 * nb,))],
        compiler_params=pltpu.CompilerParams(vmem_limit_bytes=LIMIT_P),
        cost_estimate=pl.CostEstimate(flops=0, bytes_accessed=10**6, transcendentals=0),
        name="fetch",
    )(*in_hbm(observations, outage_mask, *mats))


def deal_kernel(bits, x_ref, other_ref, mask_ref, other_mask_ref, length_ref, other_length_ref, *outs):
    cap, nblocks = mask_ref.shape
    width = length_ref.shape[1]
    half = (outs[0].shape[0] - 8) // 2
    me = lax.axis_index("tm")
    lane = lax.broadcasted_iota(jnp.int32, (cap, width), 1)
    row = lax.broadcasted_iota(jnp.int32, (cap, width), 0)
    lines = []
    for ref, length in ((mask_ref, length_ref), (other_mask_ref, other_length_ref)):
        wide = jnp.concatenate([ref[...].astype(f32)] * (width // nblocks), axis=1)
        lines.append(jnp.sum(jnp.where(lane // nblocks == row, wide, f32(0.0)), axis=0, keepdims=True))
        lines.append(length[0:1])
    meta = jnp.concatenate(lines + [jnp.zeros((4, width), f32)], axis=0)
    for k, out in enumerate(outs):
        for top in range(half // cap):
            b = held_block(me, bits, 2 * k, top)
            spot = pl.ds(pl.multiple_of(b * width, width), width)
            out[top * cap : (top + 1) * cap] = x_ref[:, spot]
            out[half + top * cap : half + (top + 1) * cap] = other_ref[:, spot]
        out[2 * half :] = meta


def join_kernel(*refs):
    out_ref = refs[-1]
    rows = refs[0].shape[0] - 8
    count = len(refs) - 1
    for k, ref in enumerate(refs[:-1]):
        out_ref[k * rows : (k + 1) * rows] = ref[:rows]
        out_ref[count * rows + 4 * k : count * rows + 4 * k + 4] = ref[rows : rows + 4]


def split_kernel(stay_ref, came_ref, *outs):
    half = outs[0].shape[0] // 2
    for k, out in enumerate(outs):
        out[:half] = stay_ref[k * half : (k + 1) * half]
        out[half:] = came_ref[k * half : (k + 1) * half]


def place_kernel(bits, *refs):
    out_ref = refs[-1]
    cap = out_ref.shape[0]
    width = refs[0].shape[1]
    tops = refs[0].shape[0] // (2 * cap)
    me = lax.axis_index("tm")
    for rel in range(1 << EXCHANGED):
        for top in range(tops):
            row = ((rel & 1) * tops + top) * cap
            b = held_block(me, bits, rel, top)
            out_ref[:, pl.ds(pl.multiple_of(b * width, width), width)] = refs[PLACED.index(rel >> 1)][row : row + cap]


def place(bits, shape, *arrays):
    vmem = pl.BlockSpec(memory_space=pltpu.VMEM)
    return pl.pallas_call(
        functools.partial(place_kernel, bits),
        out_shape=jax.ShapeDtypeStruct(shape, f32),
        in_specs=[vmem] * len(arrays),
        out_specs=vmem,
        compiler_params=pltpu.CompilerParams(vmem_limit_bytes=LIMIT_P),
        name="place",
    )(*in_vmem(*arrays))


def model_kernel(
    t_ref,
    k_ref,
    s_ref,
    after_ref,
    gain_ref,
    step_ref,
    pair_ref,
    back_ref,
    row_ref,
    col_ref,
    power_ref,
):
    nb, width = t_ref.shape[0], t_ref.shape[1]
    eye = (
        lax.broadcasted_iota(jnp.int32, (width, width), 0)
        == lax.broadcasted_iota(jnp.int32, (width, width), 1)
    ).astype(f32)
    both = range(nb)
    rt = [t_ref[j].T for j in both]
    for j in both:
        power_ref[j] = s_ref[j].T
        gain_ref[j] = right(k_ref[j])
    ru = [rt[j] - dot(left(rt[j]), gain_ref[j]) for j in both]
    u = [t_ref[j] - mul(k_ref[j], t_ref[j]) for j in both]
    for j in both:
        step_ref[j] = right(side([rt[j], ru[j]]))
    row2 = [dot(left(below([rt[j], ru[j]])), step_ref[j]) for j in both]
    col2 = [mul(below([t_ref[j], u[j]]), side([t_ref[j], u[j]])) for j in both]
    for j in both:
        back_ref[j] = right(eye - mul(rt[j], power_ref[j]))
        for a in (0, 1):
            for b in (0, 1):
                one, two = slice(a * width, (a + 1) * width), slice(b * width, (b + 1) * width)
                row_ref[j, (2 * a + b) * width : (2 * a + b + 1) * width] = row2[j][one, two]
                col_ref[j, (2 * a + b) * width : (2 * a + b + 1) * width] = col2[j][two, one]
        pair_ref[j] = right(side([row_ref[j, n * width : (n + 1) * width] for n in range(4)]))


def product_kernel(live, pair_ref, row_ref, col_ref, gain_ref, after_ref, rowprod_ref, colprod_ref, power_ref):
    nb, _, width = row_ref.shape
    levels = shift_levels(live)
    both = range(nb)
    power = [gain_ref[j] for j in both]
    for j in both:
        row4 = dot(left(row_ref[j]), pair_ref[j])
        col4 = mul(col_ref[j], side([col_ref[j, n * width : (n + 1) * width] for n in range(4)]))
        for p in range(4):
            for q in range(4):
                rowprod_ref[j, 4 * p + q] = row4[p * width : (p + 1) * width, q * width : (q + 1) * width]
                colprod_ref[j, 4 * p + q] = col4[q * width : (q + 1) * width, p * width : (p + 1) * width]
    for n, level in enumerate(levels):
        rights = [[right(power[j])] for j in both]
        if len(level) > 1:
            second = [dot(left(power[j]), rights[j][0]) for j in both]
            for j in both:
                rights[j].append(right(second[j]))
            double = [dot(left(second[j]), side(rights[j])) for j in both]
            for j in both:
                rights[j].append(right(double[j][:, :width]))
                power[j] = double[j][:, width:]
        for j in both:
            for m in range(len(level)):
                power_ref[j, n, m * 2 * width : (m + 1) * 2 * width] = rights[j][m]


def prepare(mats, after):
    nb, width = mats[0].shape[:2]
    vmem = pl.BlockSpec(memory_space=pltpu.VMEM)
    return pl.pallas_call(
        model_kernel,
        out_shape=[
            pltpu.VMEM((nb, 2 * width, width), bf16),
            pltpu.VMEM((nb, 2 * width, 2 * width), bf16),
            pltpu.VMEM((nb, 2 * width, 4 * width), bf16),
            pltpu.VMEM((nb, 2 * width, width), bf16),
            pltpu.VMEM((nb, 4 * width, width), f32),
            pltpu.VMEM((nb, 4 * width, width), f32),
            pltpu.VMEM((nb, width, width), f32),
        ],
        in_specs=[vmem] * 3 + [pl.BlockSpec(memory_space=pl.ANY)],
        out_specs=[vmem] * 7,
        compiler_params=pltpu.CompilerParams(vmem_limit_bytes=LIMIT_A),
        cost_estimate=pl.CostEstimate(flops=10**9, bytes_accessed=4 * 10**6, transcendentals=0),
        name="prepare",
    )(*in_vmem(*mats), after)


def products(live, pair, row2, col2, gain, after):
    nb, _, width = row2.shape
    levels = shift_levels(live)
    vmem = pl.BlockSpec(memory_space=pltpu.VMEM)
    return pl.pallas_call(
        functools.partial(product_kernel, live),
        out_shape=[
            pltpu.VMEM((nb, 16, width, width), f32),
            pltpu.VMEM((nb, 16, width, width), f32),
            pltpu.VMEM((nb, len(levels), 6 * width, width), bf16),
        ],
        in_specs=[vmem] * 4 + [pl.BlockSpec(memory_space=pl.ANY)],
        out_specs=[vmem] * 3,
        compiler_params=pltpu.CompilerParams(vmem_limit_bytes=LIMIT_A),
        cost_estimate=pl.CostEstimate(flops=10**9, bytes_accessed=4 * 10**6, transcendentals=0),
        name="products",
    )(*in_vmem(pair, row2, col2, gain), after)


def smoother_kernel(
    bits,
    blocks_of,
    live,
    nsent,
    *refs,
):
    smoother_body(bits, blocks_of, live, refs[:nsent], *refs[nsent:])


def smoother_body(
    bits,
    blocks_of,
    live,
    sent_refs,
    prior_ref,
    k_ref,
    step_ref,
    pair_ref,
    rowprod_ref,
    colprod_ref,
    back_ref,
    power_ref,
    stay_ref,
    leave_ref,
    gain_ref,
    seen_ref,
    col_ref,
    colgain_ref,
    start_ref,
    filt_ref,
    starts_smem,
    y_ref,
    meta_ref,
    meta_smem,
    order_ref,
    order_smem,
    sems,
):
    nb, width = gain_ref.shape[0], y_ref.shape[2]
    nblocks = prior_ref.shape[0]
    groups = 8 * y_ref.shape[0]
    cap = stay_ref.shape[0] // (4 * nb)
    meta_row = 8 * nb * cap
    nchunks = live // 4
    levels = shift_levels(live)
    blocks = blocks_of()
    me = lax.axis_index("tm")
    odd = parity(me, bits)

    part = 2 * nb * cap
    for n, ref in enumerate(sent_refs):
        spots = PARTS[n % len(PARTS)]
        for i, k in enumerate(spots):
            row = len(spots) * part + 4 * i
            y_ref[n // len(PARTS), meta_row + 4 * k : meta_row + 4 * k + 4] = ref[row : row + 4]
    meta_ref[...] = y_ref[:, meta_row:].astype(jnp.int32)
    fetch = pltpu.make_async_copy(meta_ref, meta_smem, sems.at[0])
    fetch.start()
    for n, ref in enumerate(sent_refs):
        for i, k in enumerate(PARTS[n % len(PARTS)]):
            y_ref[n // len(PARTS), k * part : (k + 1) * part] = ref[i * part : (i + 1) * part]
    places = []
    for g in range(groups):
        d = me ^ g
        places.append((d >> 3, (d >> 1) & 3, odd ^ parity(g, bits)))

    ones = jnp.ones((width, width), bf16)
    lanes = lax.broadcasted_iota(jnp.int32, (cap, width), 1)
    rows = lax.broadcasted_iota(jnp.int32, (cap, width), 0)
    packed = []
    for j, b in enumerate(blocks):
        readings = below(
            [
                y_ref[top, pl.ds(pl.multiple_of(((k * 2 + near) * nb + j) * cap, cap), cap), :]
                for top, k, near in places
            ]
        )
        gains = dot(left(readings), k_ref[j])
        chosen = lanes == rows * nblocks + b
        marks = below(
            [
                jnp.where(
                    chosen,
                    jnp.broadcast_to(y_ref[top, pl.ds(meta_row + 4 * k + 2 * near, 1), :], (cap, width)),
                    f32(0.0),
                )
                for top, k, near in places
            ]
        )
        seen = jnp.dot(marks.astype(bf16), ones, preferred_element_type=f32)
        gains = jnp.where(seen > 0.5, gains, f32(0.0))
        packed.append((gains, seen))
    fetch.wait()
    starts = [0]
    for g in range(groups):
        top, k, near = places[g]
        starts_smem[g] = starts[g]
        starts.append(starts[-1] + meta_smem[top, 4 * k + 2 * near + 1, 0])
    for j, (gains, seen) in enumerate(packed):
        for g in range(groups):
            gain_ref[j, pl.ds(starts[g], cap), :] = gains[g * cap : (g + 1) * cap]
            seen_ref[j, pl.ds(starts[g], cap), :] = seen[g * cap : (g + 1) * cap]

    gain = [[gain_ref[j, pl.ds(s, nchunks, stride=4), :] for s in range(4)] for j in range(nb)]
    marks = [[seen_ref[j, pl.ds(s, nchunks, stride=4), :] for s in range(4)] for j in range(nb)]
    for j in range(nb):
        order = ((marks[j][0] * 2.0 + marks[j][1]) * 2.0 + marks[j][2]) * 2.0 + marks[j][3]
        order_ref[j] = order.astype(jnp.int32)
    fetch = pltpu.make_async_copy(order_ref, order_smem, sems.at[1])
    fetch.start()
    seen = [[m > 0.5 for m in marks[j]] for j in range(nb)]
    begun = [
        dot(left(below([gain[j][0], gain[j][2]])), step_ref[j]) for j in range(nb)
    ]
    twos, lasts, fours = [], [], []
    for j in range(nb):
        twos.append(pick2(begun[j][:nchunks], seen[j][1], width) + gain[j][1])
        lasts.append(pick2(begun[j][nchunks:], seen[j][3], width) + gain[j][3])
    wide = [dot(left(twos[j]), pair_ref[j]) for j in range(nb)]
    for j in range(nb):
        four = pick4(wide[j], seen[j][2], seen[j][3], width) + lasts[j]
        filt_ref[j, :nchunks] = four
        pad = -nchunks % width
        padded = below([four, jnp.zeros((pad, width), f32)]) if pad else four
        for n in range(padded.shape[0] // width):
            colgain_ref[j, n] = padded[n * width : (n + 1) * width].T
        start_ref[j, pl.ds(0, 1), :] = prior_ref[pl.ds(blocks[j], 1), :]
    fetch.wait()

    lane_full = lax.broadcasted_iota(jnp.int32, (width, width), 1)

    def pattern(j, c):
        return order_smem[j, c, 0]

    def two_steps(i, state):
        moved = []
        c = 2 * i
        part = c // width
        lane = c - part * width
        here = lane_full == lane
        for j in range(nb):
            prod = colprod_ref[j, pattern(j, c)] * state[j]
            prod = prod + jnp.where(here, colgain_ref[j, part], f32(0.0))
            column = jnp.broadcast_to(jnp.sum(prod, axis=1, keepdims=True), (width, width))
            pltpu.store(col_ref.at[j, part], column, mask=here)
            row = jnp.sum(rowprod_ref[j, pattern(j, c + 1)] * column, axis=0, keepdims=True)
            row = row + filt_ref[j, pl.ds(c + 1, 1), :]
            start_ref[j, pl.ds(c + 2, 1), :] = row
            moved.append(row)
        return tuple(moved)

    lax.fori_loop(0, nchunks // 2, two_steps, tuple(prior_ref[pl.ds(b, 1), :] for b in blocks))

    for j in range(nb):
        for n in range(col_ref.shape[1]):
            count = min(width, nchunks - n * width) // 2
            flipped = col_ref[j, n].T
            col_ref[j, n] = flipped
            start_ref[j, pl.ds(n * width + 1, count, stride=2), :] = col_ref[j, n, pl.ds(0, count, stride=2), :]
    lefts = [left(start_ref[j, :nchunks]) for j in range(nb)]
    ones = [dot(lefts[j], step_ref[j]) for j in range(nb)]
    pairs = [dot(lefts[j], pair_ref[j]) for j in range(nb)]
    pairs = [pick4(pairs[j], seen[j][0], seen[j][1], width) + twos[j] for j in range(nb)]
    threes = [dot(left(pairs[j]), step_ref[j]) for j in range(nb)]
    for j in range(nb):
        one = pick2(ones[j], seen[j][0], width) + gain[j][0]
        three = pick2(threes[j], seen[j][2], width) + gain[j][2]
        four = start_ref[j, 1 : nchunks + 1]
        for s, value in enumerate((one, pairs[j], three, four)):
            filt_ref[j, pl.ds(s, nchunks, stride=4), :] = value
    is_last = lax.broadcasted_iota(jnp.int32, (live, width), 0) == live - 1
    tail = filt_ref.shape[1] - live
    filtered = [filt_ref[j, :live] for j in range(nb)]
    smoothed = [jnp.where(is_last, x, dot(left(x), back_ref[j])) for j, x in enumerate(filtered)]
    for j in range(nb):
        filt_ref[j, live:] = jnp.zeros((tail, width), f32)
    for n, level in enumerate(levels):
        for j in range(nb):
            filt_ref[j, :live] = smoothed[j]
        for j in range(nb):
            moved = side([left(filt_ref[j, sh : sh + live]) for sh in level])
            smoothed[j] = smoothed[j] + dot(moved, power_ref[j, n, : 2 * width * len(level)])
    for j in range(nb):
        filt_ref[j, :live] = smoothed[j]
    for j in range(nb):
        for d in range(1 << EXCHANGED):
            near = parity(d, EXCHANGED)
            value = filt_ref[j, pl.ds(starts_smem[me ^ d], cap), :]
            value = jnp.where(rows < meta_smem[0, 4 * (d >> 1) + 2 * near + 1, 0], value, f32(0.0))
            row = ((d >> 1) * nb + j) * cap
            (leave_ref if near else stay_ref)[row : row + cap] = value


def smooth(bits, blocks_of, nb, cap, live, sent, prior, model):
    tops = len(sent) // len(PARTS)
    width = sent[0].shape[1]
    rows = 8 * nb * cap + 16
    nchunks = live // 4
    levels = shift_levels(live)
    parts = -(-nchunks // width)
    vmem = pl.BlockSpec(memory_space=pltpu.VMEM)
    tail = max(max(level) for level in levels) + cap
    return pl.pallas_call(
        functools.partial(smoother_kernel, bits, blocks_of, live, len(sent)),
        out_shape=[pltpu.VMEM((4 * nb * cap, width), f32)] * 2,
        in_specs=[vmem] * (len(sent) + 8),
        out_specs=[vmem] * 2,
        scratch_shapes=[
            pltpu.VMEM((nb, live + cap, width), f32),
            pltpu.VMEM((nb, live + cap, width), f32),
            pltpu.VMEM((nb, parts, width, width), f32),
            pltpu.VMEM((nb, parts, width, width), f32),
            pltpu.VMEM((nb, nchunks + cap, width), f32),
            pltpu.VMEM((nb, live + tail, width), f32),
            pltpu.SMEM((8 * tops,), jnp.int32),
            pltpu.VMEM((tops, rows, width), f32),
            pltpu.VMEM((tops, 16, width), jnp.int32),
            pltpu.SMEM((tops, 16, width), jnp.int32),
            pltpu.VMEM((nb, nchunks, width), jnp.int32),
            pltpu.SMEM((nb, nchunks, width), jnp.int32),
            pltpu.SemaphoreType.DMA((2,)),
        ],
        compiler_params=pltpu.CompilerParams(vmem_limit_bytes=LIMIT_B),
        name="smooth",
    )(*in_vmem(*sent), prior, *in_vmem(*model))


def permuted(x, mask):
    count = lax.axis_size("tm")
    return lax.ppermute(x, "tm", [(i, i ^ mask) for i in range(count)])


def shards(observations, outage_mask, group_length, prior_mean, transition, filter_gain, smoother_gain):
    cap = observations.shape[0]
    nblocks, width = transition.shape[0], transition.shape[1]
    bits = lax.axis_size("tm").bit_length() - 1
    nb = nblocks >> EXCHANGED
    live = (cap << bits) * 3 // 4
    half = nb * cap

    def blocks_of():
        return [held_block(lax.axis_index("tm"), bits, 0, top) for top in range(nb)]

    masks = (3, 5, 6)
    package = (2 * half + 8, width)
    other = permuted(observations, 1), permuted(outage_mask, 1)
    length = jnp.broadcast_to(group_length.astype(f32)[:, None], (8, width))
    own = fetch(blocks_of, nb, observations, outage_mask, transition, filter_gain, smoother_gain)
    dealt = local(
        functools.partial(deal_kernel, bits),
        [package] * 4,
        "deal",
        own[0],
        other[0],
        own[1],
        other[1],
        length,
        permuted(length, 1),
    )
    crossed = [permuted(p, mask) for p, mask in zip(dealt[1:], masks)]
    held = [dealt[0], *crossed]
    sent = []
    for spots in PARTS:
        if len(spots) == 1:
            sent.append(held[spots[0]])
        else:
            rows = 2 * half * len(spots) + -(-4 * len(spots) // 8) * 8
            sent += local(join_kernel, [(rows, width)], "join", *(held[k] for k in spots))
    gain, step, pair, back, row2, col2, power = prepare(own[2:], sent[-1])
    for k in range(EXCHANGED, bits):
        sent = sent + [permuted(x, (1 << k) | 1) for x in sent]
    rowprod, colprod, powers = products(live, pair, row2, col2, power, sent[len(PARTS) - 1])
    model = [gain, step, pair, rowprod, colprod, back, powers]
    stay, leave = smooth(bits, blocks_of, nb, cap, live, sent, prior_mean.reshape(nblocks, width), model)
    split = local(split_kernel, [(2 * half, width)] * 4, "split", stay, permuted(leave, 1))
    crossed = [split[0]] + [permuted(p, mask) for p, mask in zip(split[1:], masks)]
    return place(bits, observations.shape, *(crossed[k] for k in PLACED))


def solution(mesh):
    placed = (
        P(("parts", "tm"), None),
        P(("parts", "tm"), None),
        P(("parts", "tm")),
        P("parts"),
        P(),
        P(),
        P(),
    )
    return jax.shard_map(
        shards, mesh=mesh, in_specs=placed, out_specs=P(("parts", "tm"), None), check_vma=False
    )
```

```python
import functools

import jax
import jax.numpy as jnp
from jax import lax
from jax.experimental import pallas as pl
from jax.experimental.pallas import tpu as pltpu
from jax.sharding import PartitionSpec as P

f32 = jnp.float32
bf16 = jnp.bfloat16
LIMIT_P = 2 * 1024 * 1024
LIMIT_A = 8 * 1024 * 1024
LIMIT_B = 8 * 1024 * 1024


def halves(x):
    high = x.astype(bf16)
    return high, (x - high.astype(f32)).astype(bf16)


def left(x):
    high = x.astype(bf16).astype(f32)
    both = jnp.concatenate([high, x - high], axis=0).astype(bf16)
    return jnp.concatenate([both, both], axis=1)


def right(w):
    return jnp.concatenate(halves(w), axis=0)


def dot(a, b):
    both = jnp.dot(a, b, preferred_element_type=f32)
    half = both.shape[0] // 2
    return both[:half] + both[half:]


def mul(x, w):
    return dot(left(x), right(w))


def side(mats):
    return jnp.concatenate(mats, axis=1)


def below(mats):
    return jnp.concatenate(mats, axis=0)


def pick2(wide, seen, width):
    return jnp.where(seen, wide[:, width:], wide[:, :width])


def pick4(wide, first, second, width):
    return jnp.where(
        first,
        pick2(wide[:, 2 * width :], second, width),
        pick2(wide[:, : 2 * width], second, width),
    )


def shift_levels(live):
    levels = []
    unit = 1
    while unit < live:
        levels.append([unit * m for m in (1, 2, 3) if unit * m < live])
        unit *= 4
    return levels


EXCHANGED = 3
PARTS = ((0,), (3, 1, 2))
PLACED = (0, 2, 3, 1)


def parity(value, bits):
    total = value & 1
    for k in range(1, bits):
        total = total ^ ((value >> k) & 1)
    return total


def held_block(me, bits, rel, top):
    one = ((me >> 1) & 1) ^ ((rel >> 1) & 1)
    two = ((me >> 2) & 1) ^ ((rel >> 2) & 1)
    low = parity(me, bits) ^ (rel & 1) ^ one ^ two ^ parity(top, 8)
    return low + 2 * one + 4 * two + 8 * top


def in_hbm(*arrays):
    return [pltpu.with_memory_space_constraint(a, pltpu.HBM) for a in arrays]


def in_vmem(*arrays):
    return [pltpu.with_memory_space_constraint(a, pltpu.VMEM) for a in arrays]


def local(kernel, shapes, name, *arrays):
    vmem = pl.BlockSpec(memory_space=pltpu.VMEM)
    return pl.pallas_call(
        kernel,
        out_shape=[pltpu.VMEM(shape, f32) for shape in shapes],
        in_specs=[vmem if a.dtype != bf16 else pl.BlockSpec(memory_space=pl.ANY) for a in arrays],
        out_specs=[vmem] * len(shapes),
        compiler_params=pltpu.CompilerParams(vmem_limit_bytes=LIMIT_P),
        name=name,
    )(*in_vmem(*arrays))


def fetch_kernel(blocks_of, x_hbm, mask_hbm, t_hbm, k_hbm, s_hbm, x_ref, mask_ref, t_ref, k_ref, s_ref, sems):
    copies = [
        pltpu.make_async_copy(x_hbm, x_ref, sems.at[0]),
        pltpu.make_async_copy(mask_hbm, mask_ref, sems.at[1]),
    ]
    for j, b in enumerate(blocks_of()):
        for n, (src, dst) in enumerate(((t_hbm, t_ref), (k_hbm, k_ref), (s_hbm, s_ref))):
            copies.append(pltpu.make_async_copy(src.at[b], dst.at[j], sems.at[2 + 3 * j + n]))
    for c in copies:
        c.start()
    for c in copies:
        c.wait()


def fetch(blocks_of, nb, observations, outage_mask, *mats):
    width = mats[0].shape[1]
    return pl.pallas_call(
        functools.partial(fetch_kernel, blocks_of),
        out_shape=[
            pltpu.VMEM(observations.shape, f32),
            pltpu.VMEM(outage_mask.shape, jnp.int32),
        ]
        + [pltpu.VMEM((nb, width, width), f32)] * 3,
        in_specs=[pl.BlockSpec(memory_space=pltpu.HBM)] * 5,
        out_specs=[pl.BlockSpec(memory_space=pltpu.VMEM)] * 5,
        scratch_shapes=[pltpu.SemaphoreType.DMA((2 + 3 * nb,))],
        compiler_params=pltpu.CompilerParams(vmem_limit_bytes=LIMIT_P),
        cost_estimate=pl.CostEstimate(flops=0, bytes_accessed=10**6, transcendentals=0),
        name="fetch",
    )(*in_hbm(observations, outage_mask, *mats))


def deal_kernel(bits, x_ref, other_ref, mask_ref, other_mask_ref, length_ref, other_length_ref, *outs):
    cap, nblocks = mask_ref.shape
    width = length_ref.shape[1]
    half = (outs[0].shape[0] - 8) // 2
    me = lax.axis_index("tm")
    lane = lax.broadcasted_iota(jnp.int32, (cap, width), 1)
    row = lax.broadcasted_iota(jnp.int32, (cap, width), 0)
    lines = []
    for ref, length in ((mask_ref, length_ref), (other_mask_ref, other_length_ref)):
        wide = jnp.concatenate([ref[...].astype(f32)] * (width // nblocks), axis=1)
        lines.append(jnp.sum(jnp.where(lane // nblocks == row, wide, f32(0.0)), axis=0, keepdims=True))
        lines.append(length[0:1])
    meta = jnp.concatenate(lines + [jnp.zeros((4, width), f32)], axis=0)
    for k, out in enumerate(outs):
        for top in range(half // cap):
            b = held_block(me, bits, 2 * k, top)
            spot = pl.ds(pl.multiple_of(b * width, width), width)
            out[top * cap : (top + 1) * cap] = x_ref[:, spot]
            out[half + top * cap : half + (top + 1) * cap] = other_ref[:, spot]
        out[2 * half :] = meta


def join_kernel(*refs):
    out_ref = refs[-1]
    rows = refs[0].shape[0] - 8
    count = len(refs) - 1
    for k, ref in enumerate(refs[:-1]):
        out_ref[k * rows : (k + 1) * rows] = ref[:rows]
        out_ref[count * rows + 4 * k : count * rows + 4 * k + 4] = ref[rows : rows + 4]


def split_kernel(stay_ref, came_ref, *outs):
    half = outs[0].shape[0] // 2
    for k, out in enumerate(outs):
        out[:half] = stay_ref[k * half : (k + 1) * half]
        out[half:] = came_ref[k * half : (k + 1) * half]


def place_kernel(bits, *refs):
    out_ref = refs[-1]
    cap = out_ref.shape[0]
    width = refs[0].shape[1]
    tops = refs[0].shape[0] // (2 * cap)
    me = lax.axis_index("tm")
    for rel in range(1 << EXCHANGED):
        for top in range(tops):
            row = ((rel & 1) * tops + top) * cap
            b = held_block(me, bits, rel, top)
            out_ref[:, pl.ds(pl.multiple_of(b * width, width), width)] = refs[PLACED.index(rel >> 1)][row : row + cap]


def place(bits, shape, *arrays):
    vmem = pl.BlockSpec(memory_space=pltpu.VMEM)
    return pl.pallas_call(
        functools.partial(place_kernel, bits),
        out_shape=jax.ShapeDtypeStruct(shape, f32),
        in_specs=[vmem] * len(arrays),
        out_specs=vmem,
        compiler_params=pltpu.CompilerParams(vmem_limit_bytes=LIMIT_P),
        name="place",
    )(*in_vmem(*arrays))


def model_kernel(
    t_ref,
    k_ref,
    s_ref,
    after_ref,
    gain_ref,
    step_ref,
    pair_ref,
    back_ref,
    row_ref,
    col_ref,
    power_ref,
):
    nb, width = t_ref.shape[0], t_ref.shape[1]
    eye = (
        lax.broadcasted_iota(jnp.int32, (width, width), 0)
        == lax.broadcasted_iota(jnp.int32, (width, width), 1)
    ).astype(f32)
    both = range(nb)
    rt = [t_ref[j].T for j in both]
    for j in both:
        power_ref[j] = s_ref[j].T
        gain_ref[j] = right(k_ref[j])
    ru = [rt[j] - dot(left(rt[j]), gain_ref[j]) for j in both]
    u = [t_ref[j] - mul(k_ref[j], t_ref[j]) for j in both]
    for j in both:
        step_ref[j] = right(side([rt[j], ru[j]]))
    row2 = [dot(left(below([rt[j], ru[j]])), step_ref[j]) for j in both]
    col2 = [mul(below([t_ref[j], u[j]]), side([t_ref[j], u[j]])) for j in both]
    for j in both:
        back_ref[j] = right(eye - mul(rt[j], power_ref[j]))
        for a in (0, 1):
            for b in (0, 1):
                one, two = slice(a * width, (a + 1) * width), slice(b * width, (b + 1) * width)
                row_ref[j, (2 * a + b) * width : (2 * a + b + 1) * width] = row2[j][one, two]
                col_ref[j, (2 * a + b) * width : (2 * a + b + 1) * width] = col2[j][two, one]
        pair_ref[j] = right(side([row_ref[j, n * width : (n + 1) * width] for n in range(4)]))


def product_kernel(live, pair_ref, row_ref, col_ref, gain_ref, after_ref, rowprod_ref, colprod_ref, power_ref):
    nb, _, width = row_ref.shape
    levels = shift_levels(live)
    both = range(nb)
    power = [gain_ref[j] for j in both]
    for j in both:
        row4 = dot(left(row_ref[j]), pair_ref[j])
        col4 = mul(col_ref[j], side([col_ref[j, n * width : (n + 1) * width] for n in range(4)]))
        for p in range(4):
            for q in range(4):
                rowprod_ref[j, 4 * p + q] = row4[p * width : (p + 1) * width, q * width : (q + 1) * width]
                colprod_ref[j, 4 * p + q] = col4[q * width : (q + 1) * width, p * width : (p + 1) * width]
    for n, level in enumerate(levels):
        rights = [[right(power[j])] for j in both]
        if len(level) > 1:
            second = [dot(left(power[j]), rights[j][0]) for j in both]
            for j in both:
                rights[j].append(right(second[j]))
            double = [dot(left(second[j]), side(rights[j])) for j in both]
            for j in both:
                rights[j].append(right(double[j][:, :width]))
                power[j] = double[j][:, width:]
        for j in both:
            for m in range(len(level)):
                power_ref[j, n, m * 2 * width : (m + 1) * 2 * width] = rights[j][m]


def prepare(mats, after):
    nb, width = mats[0].shape[:2]
    vmem = pl.BlockSpec(memory_space=pltpu.VMEM)
    return pl.pallas_call(
        model_kernel,
        out_shape=[
            pltpu.VMEM((nb, 2 * width, width), bf16),
            pltpu.VMEM((nb, 2 * width, 2 * width), bf16),
            pltpu.VMEM((nb, 2 * width, 4 * width), bf16),
            pltpu.VMEM((nb, 2 * width, width), bf16),
            pltpu.VMEM((nb, 4 * width, width), f32),
            pltpu.VMEM((nb, 4 * width, width), f32),
            pltpu.VMEM((nb, width, width), f32),
        ],
        in_specs=[vmem] * 3 + [pl.BlockSpec(memory_space=pl.ANY)],
        out_specs=[vmem] * 7,
        compiler_params=pltpu.CompilerParams(vmem_limit_bytes=LIMIT_A),
        cost_estimate=pl.CostEstimate(flops=10**9, bytes_accessed=4 * 10**6, transcendentals=0),
        name="prepare",
    )(*in_vmem(*mats), after)


def products(live, pair, row2, col2, gain, after):
    nb, _, width = row2.shape
    levels = shift_levels(live)
    vmem = pl.BlockSpec(memory_space=pltpu.VMEM)
    return pl.pallas_call(
        functools.partial(product_kernel, live),
        out_shape=[
            pltpu.VMEM((nb, 16, width, width), f32),
            pltpu.VMEM((nb, 16, width, width), f32),
            pltpu.VMEM((nb, len(levels), 6 * width, width), bf16),
        ],
        in_specs=[vmem] * 4 + [pl.BlockSpec(memory_space=pl.ANY)],
        out_specs=[vmem] * 3,
        compiler_params=pltpu.CompilerParams(vmem_limit_bytes=LIMIT_A),
        cost_estimate=pl.CostEstimate(flops=10**9, bytes_accessed=4 * 10**6, transcendentals=0),
        name="products",
    )(*in_vmem(pair, row2, col2, gain), after)


def smoother_kernel(
    bits,
    blocks_of,
    live,
    nsent,
    *refs,
):
    smoother_body(bits, blocks_of, live, refs[:nsent], *refs[nsent:])


def smoother_body(
    bits,
    blocks_of,
    live,
    sent_refs,
    prior_ref,
    k_ref,
    step_ref,
    pair_ref,
    rowprod_ref,
    colprod_ref,
    back_ref,
    power_ref,
    stay_ref,
    leave_ref,
    gain_ref,
    seen_ref,
    col_ref,
    colgain_ref,
    start_ref,
    filt_ref,
    starts_smem,
    y_ref,
    meta_ref,
    meta_smem,
    order_ref,
    order_smem,
    sems,
):
    nb, width = gain_ref.shape[0], y_ref.shape[2]
    nblocks = prior_ref.shape[0]
    groups = 8 * y_ref.shape[0]
    cap = stay_ref.shape[0] // (4 * nb)
    meta_row = 8 * nb * cap
    nchunks = live // 4
    levels = shift_levels(live)
    blocks = blocks_of()
    me = lax.axis_index("tm")
    odd = parity(me, bits)

    part = 2 * nb * cap
    for n, ref in enumerate(sent_refs):
        spots = PARTS[n % len(PARTS)]
        for i, k in enumerate(spots):
            row = len(spots) * part + 4 * i
            y_ref[n // len(PARTS), meta_row + 4 * k : meta_row + 4 * k + 4] = ref[row : row + 4]
    meta_ref[...] = y_ref[:, meta_row:].astype(jnp.int32)
    fetch = pltpu.make_async_copy(meta_ref, meta_smem, sems.at[0])
    fetch.start()
    for n, ref in enumerate(sent_refs):
        for i, k in enumerate(PARTS[n % len(PARTS)]):
            y_ref[n // len(PARTS), k * part : (k + 1) * part] = ref[i * part : (i + 1) * part]
    places = []
    for g in range(groups):
        d = me ^ g
        places.append((d >> 3, (d >> 1) & 3, odd ^ parity(g, bits)))

    ones = jnp.ones((width, width), bf16)
    lanes = lax.broadcasted_iota(jnp.int32, (cap, width), 1)
    rows = lax.broadcasted_iota(jnp.int32, (cap, width), 0)
    packed = []
    for j, b in enumerate(blocks):
        readings = below(
            [
                y_ref[top, pl.ds(pl.multiple_of(((k * 2 + near) * nb + j) * cap, cap), cap), :]
                for top, k, near in places
            ]
        )
        gains = dot(left(readings), k_ref[j])
        chosen = lanes == rows * nblocks + b
        marks = below(
            [
                jnp.where(
                    chosen,
                    jnp.broadcast_to(y_ref[top, pl.ds(meta_row + 4 * k + 2 * near, 1), :], (cap, width)),
                    f32(0.0),
                )
                for top, k, near in places
            ]
        )
        seen = jnp.dot(marks.astype(bf16), ones, preferred_element_type=f32)
        gains = jnp.where(seen > 0.5, gains, f32(0.0))
        packed.append((gains, seen))
    fetch.wait()
    starts = [0]
    for g in range(groups):
        top, k, near = places[g]
        starts_smem[g] = starts[g]
        starts.append(starts[-1] + meta_smem[top, 4 * k + 2 * near + 1, 0])
    for j, (gains, seen) in enumerate(packed):
        for g in range(groups):
            gain_ref[j, pl.ds(starts[g], cap), :] = gains[g * cap : (g + 1) * cap]
            seen_ref[j, pl.ds(starts[g], cap), :] = seen[g * cap : (g + 1) * cap]

    gain = [[gain_ref[j, pl.ds(s, nchunks, stride=4), :] for s in range(4)] for j in range(nb)]
    marks = [[seen_ref[j, pl.ds(s, nchunks, stride=4), :] for s in range(4)] for j in range(nb)]
    for j in range(nb):
        order = ((marks[j][0] * 2.0 + marks[j][1]) * 2.0 + marks[j][2]) * 2.0 + marks[j][3]
        order_ref[j] = order.astype(jnp.int32)
    fetch = pltpu.make_async_copy(order_ref, order_smem, sems.at[1])
    fetch.start()
    seen = [[m > 0.5 for m in marks[j]] for j in range(nb)]
    begun = [
        dot(left(below([gain[j][0], gain[j][2]])), step_ref[j]) for j in range(nb)
    ]
    twos, lasts, fours = [], [], []
    for j in range(nb):
        twos.append(pick2(begun[j][:nchunks], seen[j][1], width) + gain[j][1])
        lasts.append(pick2(begun[j][nchunks:], seen[j][3], width) + gain[j][3])
    wide = [dot(left(twos[j]), pair_ref[j]) for j in range(nb)]
    for j in range(nb):
        four = pick4(wide[j], seen[j][2], seen[j][3], width) + lasts[j]
        filt_ref[j, :nchunks] = four
        pad = -nchunks % width
        padded = below([four, jnp.zeros((pad, width), f32)]) if pad else four
        for n in range(padded.shape[0] // width):
            colgain_ref[j, n] = padded[n * width : (n + 1) * width].T
        start_ref[j, pl.ds(0, 1), :] = prior_ref[pl.ds(blocks[j], 1), :]
    fetch.wait()

    lane_full = lax.broadcasted_iota(jnp.int32, (width, width), 1)

    def pattern(j, c):
        return order_smem[j, c, 0]

    def two_steps(i, state):
        moved = []
        c = 2 * i
        part = c // width
        lane = c - part * width
        here = lane_full == lane
        for j in range(nb):
            prod = colprod_ref[j, pattern(j, c)] * state[j]
            prod = prod + jnp.where(here, colgain_ref[j, part], f32(0.0))
            column = jnp.broadcast_to(jnp.sum(prod, axis=1, keepdims=True), (width, width))
            pltpu.store(col_ref.at[j, part], column, mask=here)
            row = jnp.sum(rowprod_ref[j, pattern(j, c + 1)] * column, axis=0, keepdims=True)
            row = row + filt_ref[j, pl.ds(c + 1, 1), :]
            start_ref[j, pl.ds(c + 2, 1), :] = row
            moved.append(row)
        return tuple(moved)

    lax.fori_loop(0, nchunks // 2, two_steps, tuple(prior_ref[pl.ds(b, 1), :] for b in blocks), unroll=2)

    for j in range(nb):
        for n in range(col_ref.shape[1]):
            count = min(width, nchunks - n * width) // 2
            flipped = col_ref[j, n].T
            col_ref[j, n] = flipped
            start_ref[j, pl.ds(n * width + 1, count, stride=2), :] = col_ref[j, n, pl.ds(0, count, stride=2), :]
    lefts = [left(start_ref[j, :nchunks]) for j in range(nb)]
    ones = [dot(lefts[j], step_ref[j]) for j in range(nb)]
    pairs = [dot(lefts[j], pair_ref[j]) for j in range(nb)]
    pairs = [pick4(pairs[j], seen[j][0], seen[j][1], width) + twos[j] for j in range(nb)]
    threes = [dot(left(pairs[j]), step_ref[j]) for j in range(nb)]
    for j in range(nb):
        one = pick2(ones[j], seen[j][0], width) + gain[j][0]
        three = pick2(threes[j], seen[j][2], width) + gain[j][2]
        four = start_ref[j, 1 : nchunks + 1]
        for s, value in enumerate((one, pairs[j], three, four)):
            filt_ref[j, pl.ds(s, nchunks, stride=4), :] = value
    is_last = lax.broadcasted_iota(jnp.int32, (live, width), 0) == live - 1
    tail = filt_ref.shape[1] - live
    filtered = [filt_ref[j, :live] for j in range(nb)]
    smoothed = [jnp.where(is_last, x, dot(left(x), back_ref[j])) for j, x in enumerate(filtered)]
    for j in range(nb):
        filt_ref[j, live:] = jnp.zeros((tail, width), f32)
    for n, level in enumerate(levels):
        for j in range(nb):
            filt_ref[j, :live] = smoothed[j]
        for j in range(nb):
            reach = -(-(live - level[0]) // 8) * 8
            moved = side([left(filt_ref[j, sh : sh + reach]) for sh in level])
            moved = dot(moved, power_ref[j, n, : 2 * width * len(level)])
            if reach < live:
                moved = below([moved, jnp.zeros((live - reach, width), f32)])
            smoothed[j] = smoothed[j] + moved
    for j in range(nb):
        filt_ref[j, :live] = smoothed[j]
    for j in range(nb):
        for d in range(1 << EXCHANGED):
            near = parity(d, EXCHANGED)
            value = filt_ref[j, pl.ds(starts_smem[me ^ d], cap), :]
            value = jnp.where(rows < meta_smem[0, 4 * (d >> 1) + 2 * near + 1, 0], value, f32(0.0))
            row = ((d >> 1) * nb + j) * cap
            (leave_ref if near else stay_ref)[row : row + cap] = value


def smooth(bits, blocks_of, nb, cap, live, sent, prior, model):
    tops = len(sent) // len(PARTS)
    width = sent[0].shape[1]
    rows = 8 * nb * cap + 16
    nchunks = live // 4
    levels = shift_levels(live)
    parts = -(-nchunks // width)
    vmem = pl.BlockSpec(memory_space=pltpu.VMEM)
    tail = max(max(level) for level in levels) + cap
    return pl.pallas_call(
        functools.partial(smoother_kernel, bits, blocks_of, live, len(sent)),
        out_shape=[pltpu.VMEM((4 * nb * cap, width), f32)] * 2,
        in_specs=[vmem] * (len(sent) + 8),
        out_specs=[vmem] * 2,
        scratch_shapes=[
            pltpu.VMEM((nb, live + cap, width), f32),
            pltpu.VMEM((nb, live + cap, width), f32),
            pltpu.VMEM((nb, parts, width, width), f32),
            pltpu.VMEM((nb, parts, width, width), f32),
            pltpu.VMEM((nb, nchunks + cap, width), f32),
            pltpu.VMEM((nb, live + tail, width), f32),
            pltpu.SMEM((8 * tops,), jnp.int32),
            pltpu.VMEM((tops, rows, width), f32),
            pltpu.VMEM((tops, 16, width), jnp.int32),
            pltpu.SMEM((tops, 16, width), jnp.int32),
            pltpu.VMEM((nb, nchunks, width), jnp.int32),
            pltpu.SMEM((nb, nchunks, width), jnp.int32),
            pltpu.SemaphoreType.DMA((2,)),
        ],
        compiler_params=pltpu.CompilerParams(vmem_limit_bytes=LIMIT_B),
        name="smooth",
    )(*in_vmem(*sent), prior, *in_vmem(*model))


def permuted(x, mask):
    count = lax.axis_size("tm")
    return lax.ppermute(x, "tm", [(i, i ^ mask) for i in range(count)])


def shards(observations, outage_mask, group_length, prior_mean, transition, filter_gain, smoother_gain):
    cap = observations.shape[0]
    nblocks, width = transition.shape[0], transition.shape[1]
    bits = lax.axis_size("tm").bit_length() - 1
    nb = nblocks >> EXCHANGED
    live = (cap << bits) * 3 // 4
    half = nb * cap

    def blocks_of():
        return [held_block(lax.axis_index("tm"), bits, 0, top) for top in range(nb)]

    masks = (3, 5, 6)
    package = (2 * half + 8, width)
    other = permuted(observations, 1), permuted(outage_mask, 1)
    length = jnp.broadcast_to(group_length.astype(f32)[:, None], (8, width))
    own = fetch(blocks_of, nb, observations, outage_mask, transition, filter_gain, smoother_gain)
    dealt = local(
        functools.partial(deal_kernel, bits),
        [package] * 4,
        "deal",
        own[0],
        other[0],
        own[1],
        other[1],
        length,
        permuted(length, 1),
    )
    crossed = [permuted(p, mask) for p, mask in zip(dealt[1:], masks)]
    held = [dealt[0], *crossed]
    sent = []
    for spots in PARTS:
        if len(spots) == 1:
            sent.append(held[spots[0]])
        else:
            rows = 2 * half * len(spots) + -(-4 * len(spots) // 8) * 8
            sent += local(join_kernel, [(rows, width)], "join", *(held[k] for k in spots))
    gain, step, pair, back, row2, col2, power = prepare(own[2:], sent[-1])
    for k in range(EXCHANGED, bits):
        sent = sent + [permuted(x, (1 << k) | 1) for x in sent]
    rowprod, colprod, powers = products(live, pair, row2, col2, power, sent[len(PARTS) - 1])
    model = [gain, step, pair, rowprod, colprod, back, powers]
    stay, leave = smooth(bits, blocks_of, nb, cap, live, sent, prior_mean.reshape(nblocks, width), model)
    split = local(split_kernel, [(2 * half, width)] * 4, "split", stay, permuted(leave, 1))
    crossed = [split[0]] + [permuted(p, mask) for p, mask in zip(split[1:], masks)]
    return place(bits, observations.shape, *(crossed[k] for k in PLACED))


def solution(mesh):
    placed = (
        P(("parts", "tm"), None),
        P(("parts", "tm"), None),
        P(("parts", "tm")),
        P("parts"),
        P(),
        P(),
        P(),
    )
    return jax.shard_map(
        shards, mesh=mesh, in_specs=placed, out_specs=P(("parts", "tm"), None), check_vma=False
    )
```
